512 devices in a mesh: leaf: 512 (over z, y, x, core).
Axes of the slice: x: 4, y: 8, z: 8, core: 2. Of those that a mesh axis runs over, the one named last changes fastest.
Arguments:
- coords: bfloat16 [3, 2621440], P(None, 'leaf'), may hold values from 0 to 1
- rhs: float32 [8, 2621440], P(None, 'leaf'), may hold values from -6 to 6
- leaf_basis: bfloat16 [20480, 64, 128], P('leaf'), may hold values from -0.5 to 0.5
- leaf_transfer: bfloat16 [20480, 64, 64], P('leaf'), may hold values from -0.375 to 0.375
- upper_transfer: bfloat16 [512, 3, 64, 64], P('leaf'), may hold values from -0.25 to 0.25
- upper_coupling: bfloat16 [512, 4, 4, 64, 64], P('leaf'), may hold values from -0.1875 to 0.1875
- leaf_coupling: bfloat16 [20480, 8, 64, 64], P('leaf'), may hold values from -0.25 to 0.25
- near_lists: int32 [20480, 27], P('leaf'), may hold values from 0 to 199, as said below
- near_counts: int32 [20480], P('leaf'), may hold values from 1 to 27, as said below
- far_lists: int32 [20480, 8], P('leaf'), may hold values from 0 to 199, as said below
Outputs:
- product: float32 [8, 2621440], P(None, 'leaf')
The draws below stay inside these ranges and needn't reach their ends.
Inputs may be any that keep to these rules, and one draw needn't show every extreme that they name: `near_lists`: window indices lie within 80 of the leaf's own window index 80 + (i % 40); slot 0 is the leaf itself; both ends of the window are reached. `near_counts`: some leaf uses every slot. `far_lists`: window indices lie within 80 of the leaf's own window index and never equal it; both ends of the window are reached.
All inputs are finite; a program needn't handle non-finite values.
Results may differ from the reference program's by a relative error of at most 0.0041.
Values may be sent and summed in bfloat16 or wider, within the bound.
A program may use at most 64 MiB of HBM per device.

```python
import jax
import jax.numpy as jnp
from jax import lax

LEAF = 128
RANK = 64
NRHS = 8
LEAVES_DEV = 40
NEAR_MAX = 27
FAR_MAX = 8
CUT = 3
LEAVES = 20480
POINTS = 2621440
N_LEAF = 512


def window_lists(key, columns, skip_self):
    rows = jnp.arange(LEAVES, dtype=jnp.int32)
    local = rows % LEAVES_DEV
    centre = 2 * LEAVES_DEV + local
    if skip_self:
        first_key, second_key = jax.random.split(key)
        reach = jax.random.randint(first_key, (LEAVES, columns), 1, 2 * LEAVES_DEV + 1)
        signs = 2 * jax.random.randint(second_key, (LEAVES, columns), 0, 2) - 1
        jumps = reach * signs
    else:
        jumps = jax.random.randint(key, (LEAVES, columns), -2 * LEAVES_DEV, 2 * LEAVES_DEV + 1)
    chosen = centre[:, None] + jumps
    if not skip_self:
        chosen = chosen.at[:, 0].set(centre)
    edge = jnp.where(local == 0, 0, jnp.where(local == LEAVES_DEV - 1, 5 * LEAVES_DEV - 1, chosen[:, columns - 1]))
    chosen = chosen.at[:, columns - 1].set(edge)
    return chosen.astype(jnp.int32)


def draw_near_lists(key, part):
    key = jax.random.fold_in(key, 11)
    return window_lists(key, NEAR_MAX, False)


def draw_far_lists(key, part):
    key = jax.random.fold_in(key, 17)
    return window_lists(key, FAR_MAX, True)


def draw_near_counts(key, part):
    key = jax.random.fold_in(key, 13)
    first_key, second_key = jax.random.split(key)
    dense = jax.random.randint(first_key, (LEAVES // LEAVES_DEV,), 0, 2)
    ceiling = jnp.where(dense == 1, NEAR_MAX, max(NEAR_MAX // 3, 1))
    ceiling = jnp.repeat(ceiling, LEAVES_DEV)
    counts = jax.random.randint(second_key, (LEAVES,), 1, ceiling + 1)
    counts = counts.at[0].set(NEAR_MAX)
    return counts.astype(jnp.int32)


def level_of(stream_key, shape, shards, low, high):
    def one(dim, parts):
        steps = jax.random.uniform(jax.random.fold_in(jax.random.fold_in(stream_key, 6), dim), (parts,), jnp.float32, low / len(shards), high / len(shards))
        return jnp.repeat(jnp.exp(steps), shape[dim] // parts).reshape((-1,) + (1,) * (len(shape) - dim - 1))

    loudness = one(*shards[0])
    for cut in shards[1:]:
        loudness = loudness * one(*cut)
    return loudness


def noise(stream_key, shape, width, bound, cuts=(), held_as=jnp.bfloat16):
    result = width * jax.random.normal(stream_key, shape, jnp.float32)
    if cuts:
        result = result * level_of(stream_key, shape, cuts, -0.22, 0.18)
    return jnp.clip(result, -bound, bound).astype(held_as)


def setup_inputs(seed: int = 0) -> dict:
    keys = jax.random.split(jax.random.key(seed), 11)
    return {
        "coords": jnp.clip(1.0 * jax.random.uniform(keys[0], (3, POINTS), jnp.float32) ** level_of(keys[0], (3, POINTS), ((1, 512),), -0.2, 0.2), 0.0, 1.0).astype(jnp.bfloat16),
        "rhs": noise(keys[1], (NRHS, POINTS), 1.0, 6.0, ((1, 512),), jnp.float32),
        "leaf_basis": noise(keys[2], (LEAVES, RANK, LEAF), LEAF ** -0.5, 0.5, ((0, 512),)),
        "leaf_transfer": noise(keys[3], (LEAVES, RANK, RANK), (4 * RANK) ** -0.5, 0.375, ((0, 512),)),
        "upper_transfer": noise(keys[4], (N_LEAF, CUT, RANK, RANK), (8 * RANK) ** -0.5, 0.25, ((0, 512),)),
        "upper_coupling": noise(keys[5], (N_LEAF, CUT + 1, 4, RANK, RANK), (16 * RANK) ** -0.5, 0.1875, ((0, 512),)),
        "leaf_coupling": noise(keys[6], (LEAVES, FAR_MAX, RANK, RANK), (FAR_MAX * RANK) ** -0.5, 0.25, ((0, 512),)),
        "near_lists": draw_near_lists(jax.random.fold_in(keys[10], 71), 0),
        "near_counts": draw_near_counts(jax.random.fold_in(keys[10], 71), 0),
        "far_lists": draw_far_lists(jax.random.fold_in(keys[10], 71), 0),
    }


LENGTH_SCALE = 0.2
NOISE = 0.1
box_offsets = (-3, -2, 2, 3)

def matern(first, second):
    first = first.astype(jnp.float32)
    second = second.astype(jnp.float32)
    squared = jnp.zeros((first.shape[1], first.shape[2], second.shape[2]), jnp.float32)
    for axis_num in range(3):
        differ = first[axis_num][:, :, None] - second[axis_num][:, None, :]
        squared = squared + differ * differ
    scaled = jnp.sqrt(squared) * (3.0 ** 0.5 / LENGTH_SCALE)
    return (1.0 + scaled) * jnp.exp(-scaled)

def reference(coords, rhs, leaf_basis, leaf_transfer, upper_transfer, upper_coupling, leaf_coupling, near_lists, near_counts, far_lists):
    ndev = N_LEAF
    rhs_half = rhs.astype(jnp.bfloat16)
    coord_leaf = coords.reshape(3, LEAVES, LEAF)
    rhs_leaf = rhs_half.reshape(NRHS, LEAVES, LEAF)
    margin = 2 * LEAVES_DEV
    coord_pad = jnp.pad(coord_leaf, ((0, 0), (margin, margin), (0, 0)))
    rhs_pad = jnp.pad(rhs_leaf, ((0, 0), (margin, margin), (0, 0)))
    devices = jnp.arange(ndev, dtype=jnp.int32)

    def upsweep(device):
        start = (device * LEAVES_DEV).astype(jnp.int32)
        own_rhs = lax.dynamic_slice_in_dim(rhs_leaf, start, LEAVES_DEV, 1).astype(jnp.float32)
        basis = lax.dynamic_slice_in_dim(leaf_basis, start, LEAVES_DEV, 0).astype(jnp.float32)
        transfer = lax.dynamic_slice_in_dim(leaf_transfer, start, LEAVES_DEV, 0).astype(jnp.float32)
        coef = jnp.einsum('alp,lrp->lar', own_rhs, basis).astype(jnp.bfloat16)
        level_zero = jnp.einsum('lar,lrs->as', coef.astype(jnp.float32), transfer).astype(jnp.bfloat16)
        return (coef, level_zero)
    coef_all, level_zero = lax.map(upsweep, devices)
    coef_all = coef_all.reshape(LEAVES, NRHS, RANK)
    up_terms = jnp.einsum('das,djst->djat', level_zero.astype(jnp.float32), upper_transfer.astype(jnp.float32))
    levels = [level_zero]
    for level in range(1, CUT + 1):
        grouped = up_terms[:, level - 1].reshape(ndev >> level, 2 ** level, NRHS, RANK).sum(1)
        levels.append(grouped.astype(jnp.bfloat16))
    local = jnp.zeros((ndev, NRHS, RANK), jnp.float32)
    for level in range(CUT + 1):
        padded = jnp.pad(levels[level].astype(jnp.float32), ((3, 3), (0, 0), (0, 0)))
        own_box = jnp.right_shift(devices, level)
        for number, offset in enumerate(box_offsets):
            box_coef = padded[own_box + offset + 3]
            local = local + jnp.einsum('das,dst->dat', box_coef, upper_coupling[:, level, number].astype(jnp.float32))
    local = local.astype(jnp.bfloat16)
    coef_pad = jnp.pad(coef_all, ((margin, margin), (0, 0), (0, 0)))

    def downsweep(device):
        start = (device * LEAVES_DEV).astype(jnp.int32)
        coord_win = lax.dynamic_slice_in_dim(coord_pad, start, 5 * LEAVES_DEV, 1)
        rhs_win = lax.dynamic_slice_in_dim(rhs_pad, start, 5 * LEAVES_DEV, 1)
        coef_win = lax.dynamic_slice_in_dim(coef_pad, start, 5 * LEAVES_DEV, 0)
        own_points = lax.dynamic_slice_in_dim(coord_leaf, start, LEAVES_DEV, 1)
        near_rows = lax.dynamic_slice_in_dim(near_lists, start, LEAVES_DEV, 0)
        near_live = lax.dynamic_slice_in_dim(near_counts, start, LEAVES_DEV, 0)
        far_rows = lax.dynamic_slice_in_dim(far_lists, start, LEAVES_DEV, 0)
        basis = lax.dynamic_slice_in_dim(leaf_basis, start, LEAVES_DEV, 0).astype(jnp.float32)
        transfer = lax.dynamic_slice_in_dim(leaf_transfer, start, LEAVES_DEV, 0).astype(jnp.float32)
        coupling = lax.dynamic_slice_in_dim(leaf_coupling, start, LEAVES_DEV, 0).astype(jnp.float32)

        def one_slot(column, summed):
            chosen = near_rows[:, column]
            others = jnp.take(coord_win, chosen, axis=1)
            block = matern(own_points, others).astype(jnp.bfloat16)
            sources = jnp.take(rhs_win, chosen, axis=1)
            term = jnp.einsum('lpq,alq->alp', block.astype(jnp.float32), sources.astype(jnp.float32))
            live = (column < near_live).astype(jnp.float32)
            return summed + term * live[None, :, None]
        near = lax.fori_loop(0, NEAR_MAX, one_slot, jnp.zeros((NRHS, LEAVES_DEV, LEAF), jnp.float32))
        far_coef = jnp.take(coef_win, far_rows, axis=0).astype(jnp.float32)
        own_local = lax.dynamic_index_in_dim(local, device, 0, keepdims=False).astype(jnp.float32)
        leaf_local = jnp.einsum('lkar,lkrs->las', far_coef, coupling) + jnp.einsum('lrs,as->lar', transfer, own_local)
        leaf_local = leaf_local.astype(jnp.bfloat16)
        far = jnp.einsum('lar,lrp->alp', leaf_local.astype(jnp.float32), basis)
        return near + far
    pieces = lax.map(downsweep, devices)
    total = jnp.transpose(pieces, (1, 0, 2, 3)).reshape(NRHS, POINTS)
    return total + NOISE * rhs
```

```python
import functools
import math

import jax
import jax.numpy as jnp
from jax import lax
from jax.experimental import pallas as pl
from jax.experimental.pallas import tpu as pltpu
from jax.sharding import PartitionSpec as P

S_RATE = 3.0**0.5 / 0.2
C_RATE = S_RATE * math.log2(math.e)
NOISE = 0.1
OFFSETS = (-3, -2, 2, 3)
HALO = (-2, -1, 1, 2)
LEAVES = 40
PAIRS = LEAVES // 2
SLOTS = 27
LEVELS = 4
BATCH = 4
TINY = 1e-12
MESH = pl.DeviceIdType.MESH
bf16 = jnp.bfloat16
f32 = jnp.float32
NT = (((1,), (1,)), ((), ()))


def rounded(x):
    return x.astype(bf16).astype(f32)


def dot(a, b):
    return jnp.dot(a, b, preferred_element_type=f32)


def dot_nt(a, b):
    return lax.dot_general(a, b, NT, preferred_element_type=f32)


def norm_pieces(c):
    sq = c * c
    n2 = sq[0:1] + sq[1:2] + sq[2:3]
    high = rounded(n2)
    mid = rounded(n2 - high)
    low = n2 - high - mid
    return high, mid, low


def comm_kernel(
    coords,
    rhs,
    basis,
    transfer,
    up_t,
    up_c,
    win,
    cwin,
    pts,
    local,
    tsend,
    trecv,
    lev,
    lrecv,
    halo_send,
    halo_recv,
    chalo_send,
    chalo_recv,
    term_send,
    term_recv,
    lev_send,
    lev_recv,
):
    n = lax.axis_size("leaf")
    me = lax.axis_index("leaf")

    def away(k):
        return lax.rem(me + k + n, n)

    def partner(m):
        bits = [lax.rem(me, 2), lax.rem(me // 2, 2), lax.rem(me // 4, 2)]
        other = me
        for b in range(3):
            if m >> b & 1:
                other = other + (1 - 2 * bits[b]) * (1 << b)
        return other

    steps = sorted({abs(k) for k in HALO} | {abs(o) << j for j in range(LEVELS) for o in OFFSETS})
    barrier = pltpu.get_barrier_semaphore()
    greeted = [away(s) for s in steps] + [away(-s) for s in steps] + [partner(m) for m in range(1, 8)]
    for other in greeted:
        pl.semaphore_signal(barrier, inc=1, device_id=(other,), device_id_type=MESH)

    ones2 = jnp.ones((2, 128), f32)
    ones3 = jnp.ones((3, 128), f32)
    zero8 = jnp.zeros((8, 128), f32)

    def build(i, carry):
        at = pl.ds(pl.multiple_of(i * 128, 128), 128)
        c = coords[:, at].astype(f32)
        high, mid, low = norm_pieces(c)
        tile = jnp.concatenate([rhs[:, at], c, high, mid, low, ones2], axis=0)
        win[2 * LEAVES + i] = tile.astype(bf16)
        return carry

    lax.fori_loop(0, LEAVES, build, 0, unroll=4)
    pl.semaphore_wait(barrier, len(greeted))

    copies = []
    own = win.at[pl.ds(2 * LEAVES, LEAVES)]
    for num, k in enumerate(HALO):
        copies.append(
            pltpu.make_async_remote_copy(
                src_ref=own,
                dst_ref=win.at[pl.ds((2 - k) * LEAVES, LEAVES)],
                send_sem=halo_send.at[num],
                recv_sem=halo_recv.at[num],
                device_id=(away(k),),
                device_id_type=MESH,
            )
        )
        copies[-1].start()

    lane = lax.broadcasted_iota(jnp.int32, (8, 128), 1)

    def coef_four(u, total):
        halves = []
        for h in range(2):
            t = 2 * u + h
            at = pl.ds(pl.multiple_of(t * 256, 256), 256)
            r = rhs[:, at]
            both = jnp.concatenate([r[:, :128], r[:, 128:]], axis=0).astype(bf16)
            x = dot_nt(both, basis[t])
            pair = jnp.where(lane < 64, x[:8], x[8:])
            halves.append(pair)
            total = total + dot(pair.astype(bf16), transfer[t])
        cwin[PAIRS + u] = jnp.concatenate(halves, axis=0).astype(bf16)
        return total

    level_zero = lax.fori_loop(0, PAIRS // 2, coef_four, jnp.zeros((8, 64), f32), unroll=2)
    zero64 = jnp.zeros((8, 64), f32)

    def widen(x):
        return jnp.concatenate([x, zero64], axis=1)

    half = level_zero.astype(bf16)
    lev[0] = widen(half.astype(f32))
    for j in range(3):
        tsend[2 - j] = widen(dot(half, up_t[j]))

    terms = []
    for m in range(1, 8):
        count = 3 if m == 1 else 2 if m < 4 else 1
        terms.append(
            pltpu.make_async_remote_copy(
                src_ref=tsend.at[pl.ds(0, count)],
                dst_ref=trecv.at[m, pl.ds(0, count)],
                send_sem=term_send.at[m],
                recv_sem=term_recv.at[m],
                device_id=(partner(m),),
                device_id_type=MESH,
            )
        )
        terms[-1].start()

    def send_level(j):
        for num, o in enumerate(OFFSETS):
            copy = pltpu.make_async_remote_copy(
                src_ref=lev.at[j],
                dst_ref=lrecv.at[j, num],
                send_sem=lev_send.at[j, num],
                recv_sem=lev_recv.at[j, num],
                device_id=(away(-o * 2**j),),
                device_id_type=MESH,
            )
            copy.start()
            level_copies.append(copy)

    level_copies = []
    send_level(0)
    own_coef = cwin.at[pl.ds(PAIRS, PAIRS // 2)]
    for num, k in enumerate(HALO):
        copies.append(
            pltpu.make_async_remote_copy(
                src_ref=own_coef,
                dst_ref=cwin.at[pl.ds((2 - k) * (PAIRS // 2), PAIRS // 2)],
                send_sem=chalo_send.at[num],
                recv_sem=chalo_recv.at[num],
                device_id=(away(k),),
                device_id_type=MESH,
            )
        )
        copies[-1].start()

    for copy in terms:
        copy.wait()
    for j in (1, 2, 3):
        total = tsend[3 - j]
        for m in range(1, 2**j):
            total = total + trecv[m, 3 - j]
        lev[j] = rounded(total)
        send_level(j)

    def build_points(i, carry):
        at = pl.ds(pl.multiple_of(i * 128, 128), 128)
        c = coords[:, at].astype(f32)
        high, mid, low = norm_pieces(c)
        tile = jnp.concatenate([zero8, -2.0 * c, ones3, high, mid], axis=0)
        pts[i] = tile.T.astype(bf16)
        return carry

    lax.fori_loop(0, LEAVES, build_points, 0, unroll=4)

    for copy in level_copies:
        copy.wait()
    total = jnp.zeros((8, 64), f32)
    for j in range(LEVELS):
        for num, o in enumerate(OFFSETS):
            box = me // 2**j + o
            live = jnp.logical_and(box >= 0, box < n // 2**j)
            coef = lrecv[j, num][:, :64] * jnp.where(live, 1.0, 0.0)
            total = total + dot(coef.astype(bf16), up_c[4 * j + num])
    local[...] = total

    for copy in copies:
        copy.wait()
    for k in HALO:
        @pl.when(jnp.logical_or(me + k < 0, me + k >= n))
        def _(k=k):
            def clear(i, carry):
                win[(2 + k) * LEAVES + i] = jnp.zeros((16, 128), bf16)
                return carry

            def clear_coef(i, carry):
                cwin[(2 + k) * (PAIRS // 2) + i] = jnp.zeros((16, 128), bf16)
                return carry

            lax.fori_loop(0, LEAVES, clear, 0)
            lax.fori_loop(0, PAIRS // 2, clear_coef, 0)


def matern(u):
    u = jnp.maximum(u, TINY)
    r = u * lax.rsqrt(u)
    return ((1.0 + S_RATE * r) * jnp.exp2(-C_RATE * r)).astype(bf16)


def field_kernel(
    lists,
    counts,
    fars,
    win,
    cwin,
    pts,
    local,
    coupling,
    transfer,
    basis,
    rhs,
    out,
    table,
    *bufs,
):
    lane = lax.broadcasted_iota(jnp.int32, (8, 128), 1)
    first = lane < 64

    def expand(t, carry):
        x = cwin[t].astype(f32)
        y = pltpu.roll(x, 64, 1)
        for h in range(2):
            a, b = x[8 * h : 8 * h + 8], y[8 * h : 8 * h + 8]
            table[4 * t + 2 * h] = jnp.where(first, a, b)
            table[4 * t + 2 * h + 1] = jnp.where(first, b, a)
        return carry

    lax.fori_loop(0, 5 * PAIRS // 2, expand, 0, unroll=2)
    local_half = local[...].astype(bf16)

    def far_pair(t, carry):
        sums = []
        for h in range(2):
            i = 2 * t + h
            cols = [
                jnp.where(first, table[fars[i, 2 * m]], table[fars[i, 2 * m + 1]]) for m in range(4)
            ]
            x = jnp.concatenate(cols, axis=1).astype(bf16)
            sums.append(dot(x, coupling[i]))
        both = jnp.concatenate(sums, axis=1) + dot_nt(local_half, transfer[t])
        both = rounded(both)
        zero = jnp.zeros_like(both)
        split = jnp.concatenate([jnp.where(first, both, zero), jnp.where(first, zero, both)], axis=0)
        far = dot(split.astype(bf16), basis[t])
        for h in range(2):
            at = pl.ds(pl.multiple_of(t * 256 + h * 128, 128), 128)
            out[:, at] = far[8 * h : 8 * h + 8] + NOISE * rhs[:, at]
        return carry

    lax.fori_loop(0, PAIRS, far_pair, 0, unroll=2)

    def advance(leaf, s):
        n = counts[jnp.minimum(leaf, LEAVES - 1)]
        last = s + 2 >= n
        return jnp.where(last, leaf + 1, leaf), jnp.where(last, 0, s + 2)

    def batch_from(leaf, s):
        batch = []
        for _ in range(BATCH):
            batch.append((leaf, s))
            leaf, s = advance(leaf, s)
        return batch, leaf, s

    def entries(leaf, s):
        i = jnp.minimum(leaf, LEAVES - 1)
        return i, lists[i, s], lists[i, jnp.minimum(s + 1, SLOTS - 1)]

    def distances(batch, refs):
        for (leaf, s), ref in zip(batch, refs):
            i, a, b = entries(leaf, s)
            q = jnp.concatenate([win[a], win[b]], axis=1)
            ref[...] = dot(pts[i], q)

    def products(batch, refs):
        for (leaf, s), ref in zip(batch, refs):
            i, a, b = entries(leaf, s)
            live = leaf < LEAVES
            both = jnp.logical_and(live, s + 1 < counts[i])
            ra = jnp.where(live, win[a], jnp.zeros((16, 128), bf16))
            rb = jnp.where(both, win[b], jnp.zeros((16, 128), bf16))
            r = jnp.concatenate([ra, rb], axis=1)
            d = dot_nt(r, matern(ref[...]))
            at = pl.ds(pl.multiple_of(i * 128, 128), 128)
            out[:, at] += d[:8]

    tasks = lax.fori_loop(0, LEAVES, lambda i, t: t + (counts[i] + 1) // 2, jnp.int32(0))
    even, odd = bufs[:BATCH], bufs[BATCH:]
    zero = jnp.int32(0)
    batch, leaf, s = batch_from(zero, zero)
    distances(batch, even)

    def body(_, carry):
        first_leaf, first_s = carry
        now, leaf, s = batch_from(first_leaf, first_s)
        later, leaf2, s2 = batch_from(leaf, s)
        distances(later, odd)
        products(now, even)
        after, _, _ = batch_from(leaf2, s2)
        distances(after, even)
        products(later, odd)
        return leaf2, s2

    rounds = (tasks + 2 * BATCH - 1) // (2 * BATCH)
    lax.fori_loop(0, rounds, body, (zero, zero))


def run_field(lists, counts, fars, *arrays):
    smem = pl.BlockSpec(memory_space=pltpu.SMEM)
    vmem = pl.BlockSpec(memory_space=pltpu.VMEM)
    return pl.pallas_call(
        field_kernel,
        out_shape=jax.ShapeDtypeStruct((8, LEAVES * 128), f32),
        in_specs=[smem] * 3 + [vmem] * len(arrays),
        out_specs=vmem,
        scratch_shapes=[pltpu.VMEM((5 * LEAVES, 8, 128), f32)]
        + [pltpu.VMEM((128, 256), f32)] * (2 * BATCH),
        compiler_params=pltpu.CompilerParams(vmem_limit_bytes=40 * 2**20),
    )(lists, counts, fars, *arrays)


def run_comm(*arrays):
    vmem = pl.BlockSpec(memory_space=pltpu.VMEM)
    dma = pltpu.SemaphoreType.DMA
    return pl.pallas_call(
        comm_kernel,
        out_shape=[
            jax.ShapeDtypeStruct((5 * LEAVES, 16, 128), bf16),
            jax.ShapeDtypeStruct((5 * PAIRS // 2, 16, 128), bf16),
            jax.ShapeDtypeStruct((LEAVES, 128, 16), bf16),
            jax.ShapeDtypeStruct((8, 64), f32),
        ],
        in_specs=[vmem] * len(arrays),
        out_specs=[vmem] * 4,
        scratch_shapes=[
            pltpu.VMEM((3, 8, 128), f32),
            pltpu.VMEM((8, 3, 8, 128), f32),
            pltpu.VMEM((LEVELS, 8, 128), f32),
            pltpu.VMEM((LEVELS, 4, 8, 128), f32),
            dma((4,)),
            dma((4,)),
            dma((4,)),
            dma((4,)),
            dma((8,)),
            dma((8,)),
            dma((LEVELS, 4)),
            dma((LEVELS, 4)),
        ],
        compiler_params=pltpu.CompilerParams(
            collective_id=0, has_side_effects=True, vmem_limit_bytes=40 * 2**20
        ),
    )(*arrays)


def per_device(
    coords,
    rhs,
    leaf_basis,
    leaf_transfer,
    upper_transfer,
    upper_coupling,
    leaf_coupling,
    near_lists,
    near_counts,
    far_lists,
):
    basis = leaf_basis.reshape(PAIRS, 128, 128)
    transfer = leaf_transfer.reshape(PAIRS, 128, 64)
    coupling = leaf_coupling.reshape(LEAVES, 512, 64)
    win, cwin, pts, local = run_comm(
        coords, rhs, basis, transfer, upper_transfer[0], upper_coupling.reshape(16, 64, 64)
    )
    return run_field(
        near_lists, near_counts, far_lists, win, cwin, pts, local, coupling, transfer, basis, rhs
    )


def solution(mesh):
    return jax.shard_map(
        per_device,
        mesh=mesh,
        in_specs=(
            P(None, "leaf"),
            P(None, "leaf"),
            P("leaf", None, None),
            P("leaf", None, None),
            P("leaf", None, None, None),
            P("leaf", None, None, None, None),
            P("leaf", None, None, None),
            P("leaf", None),
            P("leaf"),
            P("leaf", None),
        ),
        out_specs=P(None, "leaf"),
        check_vma=False,
    )
```

```python
import functools
import math

import jax
import jax.numpy as jnp
from jax import lax
from jax.experimental import pallas as pl
from jax.experimental.pallas import tpu as pltpu
from jax.sharding import PartitionSpec as P

S_RATE = 3.0**0.5 / 0.2
C_RATE = S_RATE * math.log2(math.e)
NOISE = 0.1
OFFSETS = (-3, -2, 2, 3)
HALO = (-2, -1, 1, 2)
LEAVES = 40
PAIRS = LEAVES // 2
SLOTS = 27
LEVELS = 4
BATCH = 8
SIDE = 0
FAR_UNROLL = 4
TINY = 1e-12
MESH = pl.DeviceIdType.MESH
bf16 = jnp.bfloat16
f32 = jnp.float32
NT = (((1,), (1,)), ((), ()))
TN = (((0,), (0,)), ((), ()))


def rounded(x):
    return x.astype(bf16).astype(f32)


def dot(a, b):
    return jnp.dot(a, b, preferred_element_type=f32)


def dot_nt(a, b):
    return lax.dot_general(a, b, NT, preferred_element_type=f32)


def norm_pieces(c):
    sq = c * c
    n2 = sq[0:1] + sq[1:2] + sq[2:3]
    high = rounded(n2)
    mid = rounded(n2 - high)
    low = n2 - high - mid
    return high, mid, low


def comm_kernel(
    coords_h,
    rhs_h,
    basis_h,
    transfer_h,
    up_t_h,
    up_c_h,
    win,
    cwin,
    pts,
    local,
    coords,
    rhs,
    basis,
    transfer,
    up_t,
    up_c,
    load_sems,
    tsend,
    trecv,
    lev,
    lrecv,
    halo_send,
    halo_recv,
    chalo_send,
    chalo_recv,
    term_send,
    term_recv,
    lev_send,
    lev_recv,
):
    n = lax.axis_size("leaf")
    me = lax.axis_index("leaf")
    pairs = [
        (coords_h, coords),
        (rhs_h, rhs),
        (basis_h, basis),
        (transfer_h, transfer),
        (up_t_h, up_t),
        (up_c_h, up_c),
    ]
    loads = [pltpu.make_async_copy(a, b, load_sems.at[num]) for num, (a, b) in enumerate(pairs)]
    for load in loads:
        load.start()

    def away(k):
        return lax.rem(me + k + n, n)

    def partner(m):
        bits = [lax.rem(me, 2), lax.rem(me // 2, 2), lax.rem(me // 4, 2)]
        other = me
        for b in range(3):
            if m >> b & 1:
                other = other + (1 - 2 * bits[b]) * (1 << b)
        return other

    steps = sorted({abs(k) for k in HALO} | {abs(o) << j for j in range(LEVELS) for o in OFFSETS})
    barrier = pltpu.get_barrier_semaphore()
    greeted = [away(s) for s in steps] + [away(-s) for s in steps] + [partner(m) for m in range(1, 8)]
    for other in greeted:
        pl.semaphore_signal(barrier, inc=1, device_id=(other,), device_id_type=MESH)

    ones2 = jnp.ones((2, 128), f32)
    ones3 = jnp.ones((3, 128), f32)
    zero8 = jnp.zeros((8, 128), f32)

    def build(i, carry):
        at = pl.ds(pl.multiple_of(i * 128, 128), 128)
        c = coords[:, at].astype(f32)
        high, mid, low = norm_pieces(c)
        tile = jnp.concatenate([rhs[:, at], c, high, mid, low, ones2], axis=0)
        win[2 * LEAVES + i] = tile.astype(bf16)
        return carry

    for load in loads[:2]:
        load.wait()
    lax.fori_loop(0, LEAVES, build, 0, unroll=4)
    pl.semaphore_wait(barrier, len(greeted))

    copies = []
    own = win.at[pl.ds(2 * LEAVES, LEAVES)]
    for num, k in enumerate(HALO):
        copies.append(
            pltpu.make_async_remote_copy(
                src_ref=own,
                dst_ref=win.at[pl.ds((2 - k) * LEAVES, LEAVES)],
                send_sem=halo_send.at[num],
                recv_sem=halo_recv.at[num],
                device_id=(away(k),),
                device_id_type=MESH,
            )
        )
        copies[-1].start()

    lane = lax.broadcasted_iota(jnp.int32, (8, 128), 1)

    def coef_four(u, total):
        halves = []
        for h in range(2):
            t = 2 * u + h
            at = pl.ds(pl.multiple_of(t * 256, 256), 256)
            r = rhs[:, at]
            both = jnp.concatenate([r[:, :128], r[:, 128:]], axis=0).astype(bf16)
            x = dot_nt(both, basis[t])
            pair = jnp.where(lane < 64, x[:8], x[8:])
            halves.append(pair)
            total = total + dot(pair.astype(bf16), transfer[t])
        cwin[PAIRS + u] = jnp.concatenate(halves, axis=0).astype(bf16)
        return total

    for load in loads[2:]:
        load.wait()
    level_zero = lax.fori_loop(0, PAIRS // 2, coef_four, jnp.zeros((8, 64), f32), unroll=2)
    zero64 = jnp.zeros((8, 64), f32)

    def widen(x):
        return jnp.concatenate([x, zero64], axis=1)

    half = level_zero.astype(bf16)
    lev[0] = widen(half.astype(f32))
    for j in range(3):
        tsend[2 - j] = widen(dot(half, up_t[j]))

    terms = []
    for m in range(1, 8):
        count = 3 if m == 1 else 2 if m < 4 else 1
        terms.append(
            pltpu.make_async_remote_copy(
                src_ref=tsend.at[pl.ds(0, count)],
                dst_ref=trecv.at[m, pl.ds(0, count)],
                send_sem=term_send.at[m],
                recv_sem=term_recv.at[m],
                device_id=(partner(m),),
                device_id_type=MESH,
            )
        )
        terms[-1].start()

    def send_level(j):
        for num, o in enumerate(OFFSETS):
            copy = pltpu.make_async_remote_copy(
                src_ref=lev.at[j],
                dst_ref=lrecv.at[j, num],
                send_sem=lev_send.at[j, num],
                recv_sem=lev_recv.at[j, num],
                device_id=(away(-o * 2**j),),
                device_id_type=MESH,
            )
            copy.start()
            level_copies.append(copy)

    level_copies = []
    send_level(0)
    own_coef = cwin.at[pl.ds(PAIRS, PAIRS // 2)]
    for num, k in enumerate(HALO):
        copies.append(
            pltpu.make_async_remote_copy(
                src_ref=own_coef,
                dst_ref=cwin.at[pl.ds((2 - k) * (PAIRS // 2), PAIRS // 2)],
                send_sem=chalo_send.at[num],
                recv_sem=chalo_recv.at[num],
                device_id=(away(k),),
                device_id_type=MESH,
            )
        )
        copies[-1].start()

    for copy in terms:
        copy.wait()
    for j in (1, 2, 3):
        total = tsend[3 - j]
        for m in range(1, 2**j):
            total = total + trecv[m, 3 - j]
        lev[j] = rounded(total)
        send_level(j)

    def build_points(i, carry):
        at = pl.ds(pl.multiple_of(i * 128, 128), 128)
        c = coords[:, at].astype(f32)
        high, mid, low = norm_pieces(c)
        tile = jnp.concatenate([zero8, -2.0 * c, ones3, high, mid], axis=0)
        pts[i] = tile.T.astype(bf16)
        return carry

    lax.fori_loop(0, LEAVES, build_points, 0, unroll=4)

    for copy in level_copies:
        copy.wait()
    total = jnp.zeros((8, 64), f32)
    for j in range(LEVELS):
        for num, o in enumerate(OFFSETS):
            box = me // 2**j + o
            live = jnp.logical_and(box >= 0, box < n // 2**j)
            coef = lrecv[j, num][:, :64] * jnp.where(live, 1.0, 0.0)
            total = total + dot(coef.astype(bf16), up_c[4 * j + num])
    local[...] = total

    for copy in copies:
        copy.wait()
    for k in HALO:
        @pl.when(jnp.logical_or(me + k < 0, me + k >= n))
        def _(k=k):
            def clear(i, carry):
                win[(2 + k) * LEAVES + i] = jnp.zeros((16, 128), bf16)
                return carry

            def clear_coef(i, carry):
                cwin[(2 + k) * (PAIRS // 2) + i] = jnp.zeros((16, 128), bf16)
                return carry

            lax.fori_loop(0, LEAVES, clear, 0)
            lax.fori_loop(0, PAIRS // 2, clear_coef, 0)


def matern(u):
    u = jnp.maximum(u, TINY)
    r = u * lax.rsqrt(u)
    return ((1.0 + S_RATE * r) * jnp.exp2(-C_RATE * r)).astype(bf16)


def expand_coefs(cwin, table, first):
    def expand(t, carry):
        x = cwin[t].astype(f32)
        y = pltpu.roll(x, 64, 1)
        for h in range(2):
            a, b = x[8 * h : 8 * h + 8], y[8 * h : 8 * h + 8]
            table[4 * t + 2 * h] = jnp.where(first, a, b)
            table[4 * t + 2 * h + 1] = jnp.where(first, b, a)
        return carry

    lax.fori_loop(0, 5 * PAIRS // 2, expand, 0, unroll=5)


def far_phase(fars, cwin, local, coupling, transfer, basis, rhs, out, table):
    first = lax.broadcasted_iota(jnp.int32, (8, 128), 1) < 64
    expand_coefs(cwin, table, first)
    local_half = local[...].astype(bf16)

    def far_pair(t, carry):
        sums = []
        for h in range(2):
            i = 2 * t + h
            cols = [
                jnp.where(first, table[fars[2 * m, i]], table[fars[2 * m + 1, i]]) for m in range(4)
            ]
            x = jnp.concatenate(cols, axis=1).astype(bf16)
            sums.append(dot(x, coupling[i]))
        both = jnp.concatenate(sums, axis=1) + dot_nt(local_half, transfer[t])
        both = rounded(both)
        zero = jnp.zeros_like(both)
        split = jnp.concatenate([jnp.where(first, both, zero), jnp.where(first, zero, both)], axis=0)
        far = dot(split.astype(bf16), basis[t])
        for h in range(2):
            at = pl.ds(pl.multiple_of(t * 256 + h * 128, 128), 128)
            out[:, at] += far[8 * h : 8 * h + 8] + NOISE * rhs[:, at]
        return carry

    lax.fori_loop(0, PAIRS, far_pair, 0, unroll=FAR_UNROLL)


def near_phase(lists, counts, win, pts, out, dist, block):
    out[...] = jnp.zeros_like(out)
    nothing = jnp.zeros((16, 128), bf16)

    def advance(leaf, s):
        n = counts[jnp.minimum(leaf, LEAVES - 1)]
        last = s + 2 >= n
        return jnp.where(last, leaf + 1, leaf), jnp.where(last, 0, s + 2)

    def batch_from(leaf, s):
        batch = []
        for _ in range(BATCH):
            batch.append((leaf, s))
            leaf, s = advance(leaf, s)
        return batch, leaf, s

    def entries(leaf, s):
        i = jnp.minimum(leaf, LEAVES - 1)
        return i, lists[s, i], lists[jnp.minimum(s + 1, SLOTS - 1), i]

    def distance(leaf, s, g):
        i, a, b = entries(leaf, s)
        q = jnp.concatenate([win[a], win[b]], axis=1 - SIDE)
        if SIDE:
            dist[g] = lax.dot_general(q, pts[i], TN, preferred_element_type=f32)
        else:
            dist[g] = dot(pts[i], q)

    def values(g):
        block[g] = matern(dist[g])

    def product(leaf, s, g):
        i, a, b = entries(leaf, s)
        live = leaf < LEAVES
        both = jnp.logical_and(live, s + 1 < counts[i])
        ra = jnp.where(live, win[a], nothing)
        rb = jnp.where(both, win[b], nothing)
        r = jnp.concatenate([ra, rb], axis=1)
        k = block[g]
        if SIDE:
            d = dot(r, jnp.concatenate([k[:, :128], k[:, 128:]], axis=0))
        else:
            d = dot_nt(r, k)
        at = pl.ds(pl.multiple_of(i * 128, 128), 128)
        out[:, at] += d[:8]

    tasks = lax.fori_loop(0, LEAVES, lambda i, t: t + (counts[i] + 1) // 2, jnp.int32(0))
    zero = jnp.int32(0)
    now, leaf, s = batch_from(zero, zero)
    for g in range(BATCH):
        distance(*now[g], g)
    mid, leaf, s = batch_from(leaf, s)
    for g in range(BATCH):
        values(g)
        distance(*mid[g], g)

    def body(_, carry):
        now, mid, leaf, s = carry
        later, leaf, s = batch_from(leaf, s)
        for g in range(BATCH):
            product(*now[g], g)
            values(g)
            distance(*later[g], g)
        return mid, later, leaf, s

    lax.fori_loop(0, (tasks + BATCH - 1) // BATCH, body, (now, mid, leaf, s))


def field_kernel(
    lists_h,
    counts_h,
    fars_h,
    coupling_h,
    transfer_h,
    basis_h,
    rhs_h,
    win,
    cwin,
    pts,
    local,
    out,
    lists,
    counts,
    fars,
    coupling,
    transfer,
    basis,
    rhs,
    sems,
    table,
    dist,
    block,
):
    pairs = [
        (lists_h, lists),
        (counts_h, counts),
        (fars_h, fars),
        (coupling_h, coupling),
        (transfer_h, transfer),
        (basis_h, basis),
        (rhs_h, rhs),
    ]
    copies = [pltpu.make_async_copy(a, b, sems.at[n]) for n, (a, b) in enumerate(pairs)]
    for copy in copies:
        copy.start()
    for copy in copies[:2]:
        copy.wait()
    near_phase(lists, counts, win, pts, out, dist, block)
    for copy in copies[2:]:
        copy.wait()
    far_phase(fars, cwin, local, coupling, transfer, basis, rhs, out, table)


def run_field(lists, counts, fars, coupling, transfer, basis, rhs, *arrays):
    hbm = pl.BlockSpec(memory_space=pltpu.HBM)
    vmem = pl.BlockSpec(memory_space=pltpu.VMEM)
    return pl.pallas_call(
        field_kernel,
        out_shape=jax.ShapeDtypeStruct((8, LEAVES * 128), f32),
        in_specs=[hbm] * 7 + [vmem] * len(arrays),
        out_specs=vmem,
        scratch_shapes=[
            pltpu.SMEM((SLOTS, LEAVES), jnp.int32),
            pltpu.SMEM((LEAVES,), jnp.int32),
            pltpu.SMEM((8, LEAVES), jnp.int32),
            pltpu.VMEM((LEAVES, 512, 64), bf16),
            pltpu.VMEM((PAIRS, 128, 64), bf16),
            pltpu.VMEM((PAIRS, 128, 128), bf16),
            pltpu.VMEM((8, LEAVES * 128), f32),
            pltpu.SemaphoreType.DMA((7,)),
            pltpu.VMEM((5 * LEAVES, 8, 128), f32),
            pltpu.VMEM((BATCH, 128, 256), f32),
            pltpu.VMEM((BATCH, 128, 256), bf16),
        ],
        compiler_params=pltpu.CompilerParams(vmem_limit_bytes=60 * 2**20),
    )(lists, counts, fars, coupling, transfer, basis, rhs, *arrays)


def run_comm(*arrays):
    vmem = pl.BlockSpec(memory_space=pltpu.VMEM)
    hbm = pl.BlockSpec(memory_space=pltpu.HBM)
    dma = pltpu.SemaphoreType.DMA
    return pl.pallas_call(
        comm_kernel,
        out_shape=[
            jax.ShapeDtypeStruct((5 * LEAVES, 16, 128), bf16),
            jax.ShapeDtypeStruct((5 * PAIRS // 2, 16, 128), bf16),
            jax.ShapeDtypeStruct((LEAVES, 128, 16), bf16),
            jax.ShapeDtypeStruct((8, 64), f32),
        ],
        in_specs=[hbm] * len(arrays),
        out_specs=[vmem] * 4,
        scratch_shapes=[pltpu.VMEM(x.shape, x.dtype) for x in arrays]
        + [
            dma((6,)),
            pltpu.VMEM((3, 8, 128), f32),
            pltpu.VMEM((8, 3, 8, 128), f32),
            pltpu.VMEM((LEVELS, 8, 128), f32),
            pltpu.VMEM((LEVELS, 4, 8, 128), f32),
            dma((4,)),
            dma((4,)),
            dma((4,)),
            dma((4,)),
            dma((8,)),
            dma((8,)),
            dma((LEVELS, 4)),
            dma((LEVELS, 4)),
        ],
        compiler_params=pltpu.CompilerParams(
            collective_id=0, has_side_effects=True, vmem_limit_bytes=60 * 2**20
        ),
    )(*arrays)


def per_device(
    coords,
    rhs,
    leaf_basis,
    leaf_transfer,
    upper_transfer,
    upper_coupling,
    leaf_coupling,
    near_lists,
    near_counts,
    far_lists,
):
    basis = leaf_basis.reshape(PAIRS, 128, 128)
    transfer = leaf_transfer.reshape(PAIRS, 128, 64)
    coupling = leaf_coupling.reshape(LEAVES, 512, 64)
    win, cwin, pts, local = run_comm(
        coords, rhs, basis, transfer, upper_transfer[0], upper_coupling.reshape(16, 64, 64)
    )
    return run_field(
        near_lists.T, near_counts, far_lists.T, coupling, transfer, basis, rhs, win, cwin, pts, local
    )


def solution(mesh):
    return jax.shard_map(
        per_device,
        mesh=mesh,
        in_specs=(
            P(None, "leaf"),
            P(None, "leaf"),
            P("leaf", None, None),
            P("leaf", None, None),
            P("leaf", None, None, None),
            P("leaf", None, None, None, None),
            P("leaf", None, None, None),
            P("leaf", None),
            P("leaf"),
            P("leaf", None),
        ),
        out_specs=P(None, "leaf"),
        check_vma=False,
    )
```

```python
import functools
import math

import jax
import jax.numpy as jnp
from jax import lax
from jax.experimental import pallas as pl
from jax.experimental.pallas import tpu as pltpu
from jax.sharding import PartitionSpec as P

S_RATE = 3.0**0.5 / 0.2
C_RATE = S_RATE * math.log2(math.e)
NOISE = 0.1
OFFSETS = (-3, -2, 2, 3)
HALO = (-2, -1, 1, 2)
LEAVES = 40
PAIRS = LEAVES // 2
SLOTS = 27
LEVELS = 4
BATCH = 8
SIDE = 0
FAR_UNROLL = 4
COEF_UNROLL = 2
TINY = 1e-12
MESH = pl.DeviceIdType.MESH
bf16 = jnp.bfloat16
f32 = jnp.float32
NT = (((1,), (1,)), ((), ()))
TN = (((0,), (0,)), ((), ()))


def rounded(x):
    return x.astype(bf16).astype(f32)


def dot(a, b):
    return jnp.dot(a, b, preferred_element_type=f32)


def dot_nt(a, b):
    return lax.dot_general(a, b, NT, preferred_element_type=f32)


def norm_pieces(c):
    sq = c * c
    n2 = sq[0:1] + sq[1:2] + sq[2:3]
    high = rounded(n2)
    mid = rounded(n2 - high)
    low = n2 - high - mid
    return high, mid, low


def comm_kernel(
    coords_h,
    rhs_h,
    basis_h,
    transfer_h,
    up_t_h,
    up_c_h,
    win,
    cwin,
    pts,
    local,
    coords,
    rhs,
    basis,
    transfer,
    up_t,
    up_c,
    load_sems,
    tsend,
    trecv,
    lev,
    lrecv,
    halo_send,
    halo_recv,
    chalo_send,
    chalo_recv,
    term_send,
    term_recv,
    lev_send,
    lev_recv,
):
    n = lax.axis_size("leaf")
    me = lax.axis_index("leaf")
    pairs = [
        (coords_h, coords),
        (rhs_h, rhs),
        (basis_h, basis),
        (transfer_h, transfer),
        (up_t_h, up_t),
        (up_c_h, up_c),
    ]
    loads = [pltpu.make_async_copy(a, b, load_sems.at[num]) for num, (a, b) in enumerate(pairs)]
    for load in loads:
        load.start()

    def away(k):
        return lax.rem(me + k + n, n)

    def partner(m):
        bits = [lax.rem(me, 2), lax.rem(me // 2, 2), lax.rem(me // 4, 2)]
        other = me
        for b in range(3):
            if m >> b & 1:
                other = other + (1 - 2 * bits[b]) * (1 << b)
        return other

    def inside(k):
        return jnp.logical_and(me + k >= 0, me + k < n)

    steps = sorted({abs(k) for k in HALO} | {abs(o) << j for j in range(LEVELS) for o in OFFSETS})
    steps = steps + [-k for k in steps]
    lrecv[...] = jnp.zeros_like(lrecv)
    barrier = pltpu.get_barrier_semaphore()
    for m in range(1, 8):
        pl.semaphore_signal(barrier, inc=1, device_id=(partner(m),), device_id_type=MESH)
    greeted = jnp.int32(7)
    for k in steps:
        greeted = greeted + jnp.where(inside(k), 1, 0)

        @pl.when(inside(k))
        def _(k=k):
            pl.semaphore_signal(barrier, inc=1, device_id=(away(k),), device_id_type=MESH)

    ones2 = jnp.ones((2, 128), f32)
    ones3 = jnp.ones((3, 128), f32)
    zero8 = jnp.zeros((8, 128), f32)

    def build(i, carry):
        at = pl.ds(pl.multiple_of(i * 128, 128), 128)
        c = coords[:, at].astype(f32)
        high, mid, low = norm_pieces(c)
        tile = jnp.concatenate([rhs[:, at], c, high, mid, low, ones2], axis=0)
        win[2 * LEAVES + i] = tile.astype(bf16)
        return carry

    for load in loads[:2]:
        load.wait()
    lax.fori_loop(0, LEAVES, build, 0, unroll=4)

    lane = lax.broadcasted_iota(jnp.int32, (8, 128), 1)

    def coef_four(u, total):
        halves = []
        for h in range(2):
            t = 2 * u + h
            at = pl.ds(pl.multiple_of(t * 256, 256), 256)
            r = rhs[:, at]
            both = jnp.concatenate([r[:, :128], r[:, 128:]], axis=0).astype(bf16)
            x = dot_nt(both, basis[t])
            pair = jnp.where(lane < 64, x[:8], x[8:])
            halves.append(pair)
            total = total + dot(pair.astype(bf16), transfer[t])
        cwin[PAIRS + u] = jnp.concatenate(halves, axis=0).astype(bf16)
        return total

    for load in loads[2:]:
        load.wait()
    level_zero = lax.fori_loop(0, PAIRS // 2, coef_four, jnp.zeros((8, 64), f32), unroll=COEF_UNROLL)
    zero64 = jnp.zeros((8, 64), f32)

    def widen(x):
        return jnp.concatenate([x, zero64], axis=1)

    half = level_zero.astype(bf16)
    lev[0] = widen(half.astype(f32))
    for j in range(3):
        tsend[2 - j] = widen(dot(half, up_t[j]))

    for k in HALO:
        @pl.when(jnp.logical_not(inside(k)))
        def _(k=k):
            def clear(i, carry):
                win[(2 + k) * LEAVES + i] = jnp.zeros((16, 128), bf16)
                return carry

            def clear_coef(i, carry):
                cwin[(2 + k) * (PAIRS // 2) + i] = jnp.zeros((16, 128), bf16)
                return carry

            lax.fori_loop(0, LEAVES, clear, 0)
            lax.fori_loop(0, PAIRS // 2, clear_coef, 0)

    pl.semaphore_wait(barrier, greeted)

    terms = []
    for m in range(1, 8):
        count = 3 if m == 1 else 2 if m < 4 else 1
        terms.append(
            pltpu.make_async_remote_copy(
                src_ref=tsend.at[pl.ds(0, count)],
                dst_ref=trecv.at[m, pl.ds(0, count)],
                send_sem=term_send.at[m],
                recv_sem=term_recv.at[m],
                device_id=(partner(m),),
                device_id_type=MESH,
            )
        )
        terms[-1].start()

    copies = []

    def begin(k, copy):
        copies.append((k, copy))

        @pl.when(inside(k))
        def _():
            copy.start()

    def finish(some):
        for k, copy in some:
            @pl.when(inside(k))
            def _(copy=copy):
                copy.wait_send()

            @pl.when(inside(-k))
            def _(copy=copy):
                copy.wait_recv()

    def send_level(j):
        for num, o in enumerate(OFFSETS):
            k = -o * 2**j
            copy = pltpu.make_async_remote_copy(
                src_ref=lev.at[j],
                dst_ref=lrecv.at[j, num],
                send_sem=lev_send.at[j, num],
                recv_sem=lev_recv.at[j, num],
                device_id=(away(k),),
                device_id_type=MESH,
            )
            begin(k, copy)

    send_level(0)
    for ref, rows, send, recv in (
        (win, LEAVES, halo_send, halo_recv),
        (cwin, PAIRS // 2, chalo_send, chalo_recv),
    ):
        for num, k in enumerate(HALO):
            copy = pltpu.make_async_remote_copy(
                src_ref=ref.at[pl.ds(2 * rows, rows)],
                dst_ref=ref.at[pl.ds((2 - k) * rows, rows)],
                send_sem=send.at[num],
                recv_sem=recv.at[num],
                device_id=(away(k),),
                device_id_type=MESH,
            )
            begin(k, copy)

    for copy in terms:
        copy.wait()
    for j in (1, 2, 3):
        total = tsend[3 - j]
        for m in range(1, 2**j):
            total = total + trecv[m, 3 - j]
        lev[j] = rounded(total)
        send_level(j)

    def build_points(i, carry):
        at = pl.ds(pl.multiple_of(i * 128, 128), 128)
        c = coords[:, at].astype(f32)
        high, mid, low = norm_pieces(c)
        tile = jnp.concatenate([zero8, -2.0 * c, ones3, high, mid], axis=0)
        pts[i] = tile.T.astype(bf16)
        return carry

    lax.fori_loop(0, LEAVES, build_points, 0, unroll=4)

    level_copies = copies[:4] + copies[12:]
    finish(level_copies)
    total = jnp.zeros((8, 64), f32)
    for j in range(LEVELS):
        for num in range(4):
            coef = lrecv[j, num][:, :64]
            total = total + dot(coef.astype(bf16), up_c[4 * j + num])
    local[...] = total
    finish(copies[4:12])


def matern(u):
    u = jnp.maximum(u, TINY)
    r = u * lax.rsqrt(u)
    return ((1.0 + S_RATE * r) * jnp.exp2(-C_RATE * r)).astype(bf16)


def expand_coefs(cwin, table, first):
    def expand(t, carry):
        x = cwin[t].astype(f32)
        y = pltpu.roll(x, 64, 1)
        for h in range(2):
            a, b = x[8 * h : 8 * h + 8], y[8 * h : 8 * h + 8]
            table[4 * t + 2 * h] = jnp.where(first, a, b)
            table[4 * t + 2 * h + 1] = jnp.where(first, b, a)
        return carry

    lax.fori_loop(0, 5 * PAIRS // 2, expand, 0, unroll=5)


def far_phase(fars, cwin, local, coupling, transfer, basis, rhs, out, table):
    first = lax.broadcasted_iota(jnp.int32, (8, 128), 1) < 64
    expand_coefs(cwin, table, first)
    local_half = local[...].astype(bf16)

    def far_pair(t, carry):
        sums = []
        for h in range(2):
            i = 2 * t + h
            cols = [
                jnp.where(first, table[fars[2 * m, i]], table[fars[2 * m + 1, i]]) for m in range(4)
            ]
            x = jnp.concatenate(cols, axis=1).astype(bf16)
            sums.append(dot(x, coupling[i]))
        both = jnp.concatenate(sums, axis=1) + dot_nt(local_half, transfer[t])
        both = rounded(both)
        zero = jnp.zeros_like(both)
        split = jnp.concatenate([jnp.where(first, both, zero), jnp.where(first, zero, both)], axis=0)
        far = dot(split.astype(bf16), basis[t])
        for h in range(2):
            at = pl.ds(pl.multiple_of(t * 256 + h * 128, 128), 128)
            out[:, at] += far[8 * h : 8 * h + 8] + NOISE * rhs[:, at]
        return carry

    lax.fori_loop(0, PAIRS, far_pair, 0, unroll=FAR_UNROLL)


def near_phase(lists, counts, win, pts, out, dist, block):
    out[...] = jnp.zeros_like(out)
    nothing = jnp.zeros((16, 128), bf16)

    def advance(leaf, s):
        n = counts[jnp.minimum(leaf, LEAVES - 1)]
        last = s + 2 >= n
        return jnp.where(last, leaf + 1, leaf), jnp.where(last, 0, s + 2)

    def batch_from(leaf, s):
        batch = []
        for _ in range(BATCH):
            batch.append((leaf, s))
            leaf, s = advance(leaf, s)
        return batch, leaf, s

    def entries(leaf, s):
        i = jnp.minimum(leaf, LEAVES - 1)
        return i, lists[s, i], lists[jnp.minimum(s + 1, SLOTS - 1), i]

    def distance(leaf, s, g):
        i, a, b = entries(leaf, s)
        q = jnp.concatenate([win[a], win[b]], axis=1 - SIDE)
        if SIDE:
            dist[g] = lax.dot_general(q, pts[i], TN, preferred_element_type=f32)
        else:
            dist[g] = dot(pts[i], q)

    def values(g):
        block[g] = matern(dist[g])

    def product(leaf, s, g):
        i, a, b = entries(leaf, s)
        live = leaf < LEAVES
        both = jnp.logical_and(live, s + 1 < counts[i])
        ra = jnp.where(live, win[a], nothing)
        rb = jnp.where(both, win[b], nothing)
        r = jnp.concatenate([ra, rb], axis=1)
        k = block[g]
        if SIDE:
            d = dot(r, jnp.concatenate([k[:, :128], k[:, 128:]], axis=0))
        else:
            d = dot_nt(r, k)
        at = pl.ds(pl.multiple_of(i * 128, 128), 128)
        out[:, at] += d[:8]

    tasks = lax.fori_loop(0, LEAVES, lambda i, t: t + (counts[i] + 1) // 2, jnp.int32(0))
    zero = jnp.int32(0)
    now, leaf, s = batch_from(zero, zero)
    for g in range(BATCH):
        distance(*now[g], g)
    mid, leaf, s = batch_from(leaf, s)
    for g in range(BATCH):
        values(g)
        distance(*mid[g], g)

    def body(_, carry):
        now, mid, leaf, s = carry
        later, leaf, s = batch_from(leaf, s)
        for g in range(BATCH):
            product(*now[g], g)
            values(g)
            distance(*later[g], g)
        return mid, later, leaf, s

    lax.fori_loop(0, (tasks + BATCH - 1) // BATCH, body, (now, mid, leaf, s))


def field_kernel(
    lists_h,
    counts_h,
    fars_h,
    coupling_h,
    transfer_h,
    basis_h,
    rhs_h,
    win,
    cwin,
    pts,
    local,
    out,
    lists,
    counts,
    fars,
    coupling,
    transfer,
    basis,
    rhs,
    sems,
    table,
    dist,
    block,
):
    pairs = [
        (lists_h, lists),
        (counts_h, counts),
        (fars_h, fars),
        (coupling_h, coupling),
        (transfer_h, transfer),
        (basis_h, basis),
        (rhs_h, rhs),
    ]
    copies = [pltpu.make_async_copy(a, b, sems.at[n]) for n, (a, b) in enumerate(pairs)]
    for copy in copies:
        copy.start()
    for copy in copies[:2]:
        copy.wait()
    near_phase(lists, counts, win, pts, out, dist, block)
    for copy in copies[2:]:
        copy.wait()
    far_phase(fars, cwin, local, coupling, transfer, basis, rhs, out, table)


def run_field(lists, counts, fars, coupling, transfer, basis, rhs, *arrays):
    hbm = pl.BlockSpec(memory_space=pltpu.HBM)
    vmem = pl.BlockSpec(memory_space=pltpu.VMEM)
    return pl.pallas_call(
        field_kernel,
        out_shape=jax.ShapeDtypeStruct((8, LEAVES * 128), f32),
        in_specs=[hbm] * 7 + [vmem] * len(arrays),
        out_specs=vmem,
        scratch_shapes=[
            pltpu.SMEM((SLOTS, LEAVES), jnp.int32),
            pltpu.SMEM((LEAVES,), jnp.int32),
            pltpu.SMEM((8, LEAVES), jnp.int32),
            pltpu.VMEM((LEAVES, 512, 64), bf16),
            pltpu.VMEM((PAIRS, 128, 64), bf16),
            pltpu.VMEM((PAIRS, 128, 128), bf16),
            pltpu.VMEM((8, LEAVES * 128), f32),
            pltpu.SemaphoreType.DMA((7,)),
            pltpu.VMEM((5 * LEAVES, 8, 128), f32),
            pltpu.VMEM((BATCH, 128, 256), f32),
            pltpu.VMEM((BATCH, 128, 256), bf16),
        ],
        compiler_params=pltpu.CompilerParams(vmem_limit_bytes=60 * 2**20),
    )(lists, counts, fars, coupling, transfer, basis, rhs, *arrays)


def run_comm(*arrays):
    vmem = pl.BlockSpec(memory_space=pltpu.VMEM)
    hbm = pl.BlockSpec(memory_space=pltpu.HBM)
    dma = pltpu.SemaphoreType.DMA
    return pl.pallas_call(
        comm_kernel,
        out_shape=[
            jax.ShapeDtypeStruct((5 * LEAVES, 16, 128), bf16),
            jax.ShapeDtypeStruct((5 * PAIRS // 2, 16, 128), bf16),
            jax.ShapeDtypeStruct((LEAVES, 128, 16), bf16),
            jax.ShapeDtypeStruct((8, 64), f32),
        ],
        in_specs=[hbm] * len(arrays),
        out_specs=[vmem] * 4,
        scratch_shapes=[pltpu.VMEM(x.shape, x.dtype) for x in arrays]
        + [
            dma((6,)),
            pltpu.VMEM((3, 8, 128), f32),
            pltpu.VMEM((8, 3, 8, 128), f32),
            pltpu.VMEM((LEVELS, 8, 128), f32),
            pltpu.VMEM((LEVELS, 4, 8, 128), f32),
            dma((4,)),
            dma((4,)),
            dma((4,)),
            dma((4,)),
            dma((8,)),
            dma((8,)),
            dma((LEVELS, 4)),
            dma((LEVELS, 4)),
        ],
        compiler_params=pltpu.CompilerParams(
            collective_id=0, has_side_effects=True, vmem_limit_bytes=60 * 2**20
        ),
    )(*arrays)


def per_device(
    coords,
    rhs,
    leaf_basis,
    leaf_transfer,
    upper_transfer,
    upper_coupling,
    leaf_coupling,
    near_lists,
    near_counts,
    far_lists,
):
    basis = leaf_basis.reshape(PAIRS, 128, 128)
    transfer = leaf_transfer.reshape(PAIRS, 128, 64)
    coupling = leaf_coupling.reshape(LEAVES, 512, 64)
    win, cwin, pts, local = run_comm(
        coords, rhs, basis, transfer, upper_transfer[0], upper_coupling.reshape(16, 64, 64)
    )
    return run_field(
        near_lists.T, near_counts, far_lists.T, coupling, transfer, basis, rhs, win, cwin, pts, local
    )


def solution(mesh):
    return jax.shard_map(
        per_device,
        mesh=mesh,
        in_specs=(
            P(None, "leaf"),
            P(None, "leaf"),
            P("leaf", None, None),
            P("leaf", None, None),
            P("leaf", None, None, None),
            P("leaf", None, None, None, None),
            P("leaf", None, None, None),
            P("leaf", None),
            P("leaf"),
            P("leaf", None),
        ),
        out_specs=P(None, "leaf"),
        check_vma=False,
    )
```

```python
import functools
import math

import jax
import jax.numpy as jnp
from jax import lax
from jax.experimental import pallas as pl
from jax.experimental.pallas import tpu as pltpu
from jax.sharding import PartitionSpec as P

S_RATE = 3.0**0.5 / 0.2
C_RATE = S_RATE * math.log2(math.e)
NOISE = 0.1
OFFSETS = (-3, -2, 2, 3)
HALO = (-2, -1, 1, 2)
LEAVES = 40
PAIRS = LEAVES // 2
SLOTS = 27
LEVELS = 4
BATCH = 8
SIDE = 0
COEF_UNROLL = 2
TINY = 1e-12
MESH = pl.DeviceIdType.MESH
bf16 = jnp.bfloat16
f32 = jnp.float32
NT = (((1,), (1,)), ((), ()))
TN = (((0,), (0,)), ((), ()))


def rounded(x):
    return x.astype(bf16).astype(f32)


def dot(a, b):
    return jnp.dot(a, b, preferred_element_type=f32)


def dot_nt(a, b):
    return lax.dot_general(a, b, NT, preferred_element_type=f32)


def norm_pieces(c):
    sq = c * c
    n2 = sq[0:1] + sq[1:2] + sq[2:3]
    high = rounded(n2)
    mid = rounded(n2 - high)
    low = n2 - high - mid
    return high, mid, low


def comm_kernel(
    coords_h,
    rhs_h,
    basis_h,
    transfer_h,
    up_t_h,
    up_c_h,
    win,
    cwin,
    pts_h,
    local_h,
    coords,
    rhs,
    basis,
    transfer,
    up_t,
    up_c,
    load_sems,
    own,
    cown,
    pts,
    local,
    blank,
    store_sems,
    blank_sems,
    tsend,
    trecv,
    lev,
    lrecv,
    halo_send,
    halo_recv,
    chalo_send,
    chalo_recv,
    term_send,
    term_recv,
    lev_send,
    lev_recv,
):
    n = lax.axis_size("leaf")
    me = lax.axis_index("leaf")
    pairs = [
        (coords_h, coords),
        (rhs_h, rhs),
        (basis_h, basis),
        (transfer_h, transfer),
        (up_t_h, up_t),
        (up_c_h, up_c),
    ]
    loads = [pltpu.make_async_copy(a, b, load_sems.at[num]) for num, (a, b) in enumerate(pairs)]
    for load in loads:
        load.start()

    def away(k):
        return lax.rem(me + k + n, n)

    def partner(m):
        bits = [lax.rem(me, 2), lax.rem(me // 2, 2), lax.rem(me // 4, 2)]
        other = me
        for b in range(3):
            if m >> b & 1:
                other = other + (1 - 2 * bits[b]) * (1 << b)
        return other

    def inside(k):
        return jnp.logical_and(me + k >= 0, me + k < n)

    steps = sorted({abs(k) for k in HALO} | {abs(o) << j for j in range(LEVELS) for o in OFFSETS})
    steps = steps + [-k for k in steps]
    lrecv[...] = jnp.zeros_like(lrecv)
    barrier = pltpu.get_barrier_semaphore()
    for m in range(1, 8):
        pl.semaphore_signal(barrier, inc=1, device_id=(partner(m),), device_id_type=MESH)
    greeted = jnp.int32(7)
    for k in steps:
        greeted = greeted + jnp.where(inside(k), 1, 0)

        @pl.when(inside(k))
        def _(k=k):
            pl.semaphore_signal(barrier, inc=1, device_id=(away(k),), device_id_type=MESH)

    ones2 = jnp.ones((2, 128), f32)
    ones3 = jnp.ones((3, 128), f32)
    zero8 = jnp.zeros((8, 128), f32)

    def build(i, carry):
        at = pl.ds(pl.multiple_of(i * 128, 128), 128)
        c = coords[:, at].astype(f32)
        high, mid, low = norm_pieces(c)
        tile = jnp.concatenate([rhs[:, at], c, high, mid, low, ones2], axis=0)
        own[i] = tile.astype(bf16)
        return carry

    for load in loads[:2]:
        load.wait()
    lax.fori_loop(0, LEAVES, build, 0, unroll=4)

    lane = lax.broadcasted_iota(jnp.int32, (8, 128), 1)

    def coef_four(u, total):
        halves = []
        for h in range(2):
            t = 2 * u + h
            at = pl.ds(pl.multiple_of(t * 256, 256), 256)
            r = rhs[:, at]
            both = jnp.concatenate([r[:, :128], r[:, 128:]], axis=0).astype(bf16)
            x = dot_nt(both, basis[t])
            pair = jnp.where(lane < 64, x[:8], x[8:])
            halves.append(pair)
            total = total + dot(pair.astype(bf16), transfer[t])
        cown[u] = jnp.concatenate(halves, axis=0).astype(bf16)
        return total

    for load in loads[2:]:
        load.wait()
    level_zero = lax.fori_loop(0, PAIRS // 2, coef_four, jnp.zeros((8, 64), f32), unroll=COEF_UNROLL)
    zero64 = jnp.zeros((8, 64), f32)

    def widen(x):
        return jnp.concatenate([x, zero64], axis=1)

    half = level_zero.astype(bf16)
    lev[0] = widen(half.astype(f32))
    for j in range(3):
        tsend[2 - j] = widen(dot(half, up_t[j]))

    blank[...] = jnp.zeros_like(blank)
    stores = [
        pltpu.make_async_copy(own, win.at[pl.ds(2 * LEAVES, LEAVES)], store_sems.at[0]),
        pltpu.make_async_copy(cown, cwin.at[pl.ds(PAIRS, PAIRS // 2)], store_sems.at[1]),
    ]
    for store in stores:
        store.start()

    def clears(num, k):
        return (
            pltpu.make_async_copy(
                blank, win.at[pl.ds((2 + k) * LEAVES, LEAVES)], blank_sems.at[num, 0]
            ),
            pltpu.make_async_copy(
                blank.at[pl.ds(0, PAIRS // 2)],
                cwin.at[pl.ds((2 + k) * (PAIRS // 2), PAIRS // 2)],
                blank_sems.at[num, 1],
            ),
        )

    for num, k in enumerate(HALO):
        @pl.when(jnp.logical_not(inside(k)))
        def _(num=num, k=k):
            for clear in clears(num, k):
                clear.start()

    pl.semaphore_wait(barrier, greeted)

    terms = []
    for m in range(1, 8):
        count = 3 if m == 1 else 2 if m < 4 else 1
        terms.append(
            pltpu.make_async_remote_copy(
                src_ref=tsend.at[pl.ds(0, count)],
                dst_ref=trecv.at[m, pl.ds(0, count)],
                send_sem=term_send.at[m],
                recv_sem=term_recv.at[m],
                device_id=(partner(m),),
                device_id_type=MESH,
            )
        )
        terms[-1].start()

    copies = []

    def begin(k, copy):
        copies.append((k, copy))

        @pl.when(inside(k))
        def _():
            copy.start()

    def finish(some):
        for k, copy in some:
            @pl.when(inside(k))
            def _(copy=copy):
                copy.wait_send()

            @pl.when(inside(-k))
            def _(copy=copy):
                copy.wait_recv()

    def send_level(j):
        for num, o in enumerate(OFFSETS):
            k = -o * 2**j
            copy = pltpu.make_async_remote_copy(
                src_ref=lev.at[j],
                dst_ref=lrecv.at[j, num],
                send_sem=lev_send.at[j, num],
                recv_sem=lev_recv.at[j, num],
                device_id=(away(k),),
                device_id_type=MESH,
            )
            begin(k, copy)

    send_level(0)
    for mine, ref, rows, send, recv in (
        (own, win, LEAVES, halo_send, halo_recv),
        (cown, cwin, PAIRS // 2, chalo_send, chalo_recv),
    ):
        for num, k in enumerate(HALO):
            copy = pltpu.make_async_remote_copy(
                src_ref=mine,
                dst_ref=ref.at[pl.ds((2 - k) * rows, rows)],
                send_sem=send.at[num],
                recv_sem=recv.at[num],
                device_id=(away(k),),
                device_id_type=MESH,
            )
            begin(k, copy)

    for copy in terms:
        copy.wait()
    for j in (1, 2, 3):
        total = tsend[3 - j]
        for m in range(1, 2**j):
            total = total + trecv[m, 3 - j]
        lev[j] = rounded(total)
        send_level(j)

    def build_points(i, carry):
        at = pl.ds(pl.multiple_of(i * 128, 128), 128)
        c = coords[:, at].astype(f32)
        high, mid, low = norm_pieces(c)
        tile = jnp.concatenate([zero8, -2.0 * c, ones3, high, mid], axis=0)
        pts[i] = tile.T.astype(bf16)
        return carry

    lax.fori_loop(0, LEAVES, build_points, 0, unroll=4)
    stores.append(pltpu.make_async_copy(pts, pts_h, store_sems.at[2]))
    stores[-1].start()

    level_copies = copies[:4] + copies[12:]
    finish(level_copies)
    total = jnp.zeros((8, 64), f32)
    for j in range(LEVELS):
        for num in range(4):
            coef = lrecv[j, num][:, :64]
            total = total + dot(coef.astype(bf16), up_c[4 * j + num])
    local[...] = total
    stores.append(pltpu.make_async_copy(local, local_h, store_sems.at[3]))
    stores[-1].start()
    for store in stores:
        store.wait()
    for num, k in enumerate(HALO):
        @pl.when(jnp.logical_not(inside(k)))
        def _(num=num, k=k):
            for clear in clears(num, k):
                clear.wait()

    finish(copies[4:12])


def matern(u):
    u = jnp.maximum(u, TINY)
    r = u * lax.rsqrt(u)
    return ((1.0 + S_RATE * r) * jnp.exp2(-C_RATE * r)).astype(bf16)


def expand_coefs(cwin, table, first):
    def expand(t, carry):
        x = cwin[t].astype(f32)
        y = pltpu.roll(x, 64, 1)
        for h in range(2):
            a, b = x[8 * h : 8 * h + 8], y[8 * h : 8 * h + 8]
            table[4 * t + 2 * h] = jnp.where(first, a, b)
            table[4 * t + 2 * h + 1] = jnp.where(first, b, a)
        return carry

    lax.fori_loop(0, 5 * PAIRS // 2, expand, 0, unroll=5)


def far_stage(fars, cwin, local, coupling, transfer, basis, rhs, out, table, held):
    first = lax.broadcasted_iota(jnp.int32, (8, 128), 1) < 64
    expand_coefs(cwin, table, first)
    local_half = local[...].astype(bf16)

    def far_sums(t):
        sums = []
        for h in range(2):
            i = 2 * t + h
            cols = [
                jnp.where(first, table[fars[2 * m, i]], table[fars[2 * m + 1, i]]) for m in range(4)
            ]
            x = jnp.concatenate(cols, axis=1).astype(bf16)
            sums.append(dot(x, coupling[i]))
        both = jnp.concatenate(sums, axis=1) + dot_nt(local_half, transfer[t])
        held[...] = rounded(both)

    def far_field(t):
        both = held[...]
        zero = jnp.zeros_like(both)
        split = jnp.concatenate([jnp.where(first, both, zero), jnp.where(first, zero, both)], axis=0)
        far = dot(split.astype(bf16), basis[t])
        for h in range(2):
            at = pl.ds(pl.multiple_of(t * 256 + h * 128, 128), 128)
            out[:, at] += far[8 * h : 8 * h + 8] + NOISE * rhs[:, at]

    return far_sums, far_field


def field_phase(lists, counts, win, pts, out, dist, block, prepare_far):
    out[...] = jnp.zeros_like(out)
    nothing = jnp.zeros((16, 128), bf16)

    def advance(leaf, s):
        n = counts[jnp.minimum(leaf, LEAVES - 1)]
        last = s + 2 >= n
        return jnp.where(last, leaf + 1, leaf), jnp.where(last, 0, s + 2)

    def batch_from(leaf, s):
        batch = []
        for _ in range(BATCH):
            batch.append((leaf, s))
            leaf, s = advance(leaf, s)
        return batch, leaf, s

    def entries(leaf, s):
        i = jnp.minimum(leaf, LEAVES - 1)
        return i, lists[s, i], lists[jnp.minimum(s + 1, SLOTS - 1), i]

    def distance(leaf, s, g):
        i, a, b = entries(leaf, s)
        q = jnp.concatenate([win[a], win[b]], axis=1 - SIDE)
        if SIDE:
            dist[g] = lax.dot_general(q, pts[i], TN, preferred_element_type=f32)
        else:
            dist[g] = dot(pts[i], q)

    def values(g):
        block[g] = matern(dist[g])

    def product(leaf, s, g):
        i, a, b = entries(leaf, s)
        live = leaf < LEAVES
        both = jnp.logical_and(live, s + 1 < counts[i])
        ra = jnp.where(live, win[a], nothing)
        rb = jnp.where(both, win[b], nothing)
        r = jnp.concatenate([ra, rb], axis=1)
        k = block[g]
        if SIDE:
            d = dot(r, jnp.concatenate([k[:, :128], k[:, 128:]], axis=0))
        else:
            d = dot_nt(r, k)
        at = pl.ds(pl.multiple_of(i * 128, 128), 128)
        out[:, at] += d[:8]

    tasks = lax.fori_loop(0, LEAVES, lambda i, t: t + (counts[i] + 1) // 2, jnp.int32(0))
    zero = jnp.int32(0)
    now, leaf, s = batch_from(zero, zero)
    for g in range(BATCH):
        distance(*now[g], g)
    mid, leaf, s = batch_from(leaf, s)
    for g in range(BATCH):
        values(g)
        distance(*mid[g], g)

    def near_step(carry, extra=None):
        now, mid, leaf, s = carry
        later, leaf, s = batch_from(leaf, s)
        for g in range(BATCH):
            if extra and g in extra:
                extra[g]()
            product(*now[g], g)
            values(g)
            distance(*later[g], g)
        return mid, later, leaf, s

    rounds = (tasks + BATCH - 1) // BATCH
    shared = jnp.minimum(rounds, PAIRS)
    carry = lax.fori_loop(0, rounds - shared, lambda _, c: near_step(c), (now, mid, leaf, s))
    far_sums, far_field = prepare_far()

    def both_steps(t, carry):
        return near_step(carry, {1: lambda: far_sums(t), 7: lambda: far_field(t)})

    def far_step(t, carry):
        far_sums(t)
        far_field(t)
        return carry

    lax.fori_loop(0, shared, both_steps, carry)
    lax.fori_loop(shared, PAIRS, far_step, 0)


def field_kernel(
    lists_h,
    counts_h,
    fars_h,
    coupling_h,
    transfer_h,
    basis_h,
    rhs_h,
    win_h,
    cwin_h,
    pts_h,
    local_h,
    out,
    lists,
    counts,
    fars,
    coupling,
    transfer,
    basis,
    rhs,
    win,
    cwin,
    pts,
    local,
    sems,
    table,
    held,
    dist,
    block,
):
    pairs = [
        (lists_h, lists),
        (counts_h, counts),
        (win_h, win),
        (pts_h, pts),
        (fars_h, fars),
        (cwin_h, cwin),
        (local_h, local),
        (coupling_h, coupling),
        (transfer_h, transfer),
        (basis_h, basis),
        (rhs_h, rhs),
    ]
    copies = [pltpu.make_async_copy(a, b, sems.at[n]) for n, (a, b) in enumerate(pairs)]
    for copy in copies[:4]:
        copy.start()
    for copy in copies[:4]:
        copy.wait()
    for copy in copies[4:]:
        copy.start()
    def prepare_far():
        for copy in copies[4:]:
            copy.wait()
        return far_stage(fars, cwin, local, coupling, transfer, basis, rhs, out, table, held)

    field_phase(lists, counts, win, pts, out, dist, block, prepare_far)


def run_field(lists, counts, fars, coupling, transfer, basis, rhs, *arrays):
    hbm = pl.BlockSpec(memory_space=pltpu.HBM)
    vmem = pl.BlockSpec(memory_space=pltpu.VMEM)
    return pl.pallas_call(
        field_kernel,
        out_shape=jax.ShapeDtypeStruct((8, LEAVES * 128), f32),
        in_specs=[hbm] * (7 + len(arrays)),
        out_specs=vmem,
        scratch_shapes=[
            pltpu.SMEM((SLOTS, LEAVES), jnp.int32),
            pltpu.SMEM((LEAVES,), jnp.int32),
            pltpu.SMEM((8, LEAVES), jnp.int32),
            pltpu.VMEM((LEAVES, 512, 64), bf16),
            pltpu.VMEM((PAIRS, 128, 64), bf16),
            pltpu.VMEM((PAIRS, 128, 128), bf16),
            pltpu.VMEM((8, LEAVES * 128), f32),
            *[pltpu.VMEM(x.shape, x.dtype) for x in arrays],
            pltpu.SemaphoreType.DMA((11,)),
            pltpu.VMEM((5 * LEAVES, 8, 128), f32),
            pltpu.VMEM((8, 128), f32),
            pltpu.VMEM((BATCH, 128, 256), f32),
            pltpu.VMEM((BATCH, 128, 256), bf16),
        ],
        compiler_params=pltpu.CompilerParams(vmem_limit_bytes=60 * 2**20),
    )(lists, counts, fars, coupling, transfer, basis, rhs, *arrays)


def run_comm(*arrays):
    hbm = pl.BlockSpec(memory_space=pltpu.HBM)
    dma = pltpu.SemaphoreType.DMA
    return pl.pallas_call(
        comm_kernel,
        out_shape=[
            jax.ShapeDtypeStruct((5 * LEAVES, 16, 128), bf16),
            jax.ShapeDtypeStruct((5 * PAIRS // 2, 16, 128), bf16),
            jax.ShapeDtypeStruct((LEAVES, 128, 16), bf16),
            jax.ShapeDtypeStruct((8, 64), f32),
        ],
        in_specs=[hbm] * len(arrays),
        out_specs=[hbm] * 4,
        scratch_shapes=[pltpu.VMEM(x.shape, x.dtype) for x in arrays]
        + [
            dma((6,)),
            pltpu.VMEM((LEAVES, 16, 128), bf16),
            pltpu.VMEM((PAIRS // 2, 16, 128), bf16),
            pltpu.VMEM((LEAVES, 128, 16), bf16),
            pltpu.VMEM((8, 64), f32),
            pltpu.VMEM((LEAVES, 16, 128), bf16),
            dma((4,)),
            dma((4, 2)),
            pltpu.VMEM((3, 8, 128), f32),
            pltpu.VMEM((8, 3, 8, 128), f32),
            pltpu.VMEM((LEVELS, 8, 128), f32),
            pltpu.VMEM((LEVELS, 4, 8, 128), f32),
            dma((4,)),
            dma((4,)),
            dma((4,)),
            dma((4,)),
            dma((8,)),
            dma((8,)),
            dma((LEVELS, 4)),
            dma((LEVELS, 4)),
        ],
        compiler_params=pltpu.CompilerParams(
            collective_id=0, has_side_effects=True, vmem_limit_bytes=60 * 2**20
        ),
    )(*arrays)


def per_device(
    coords,
    rhs,
    leaf_basis,
    leaf_transfer,
    upper_transfer,
    upper_coupling,
    leaf_coupling,
    near_lists,
    near_counts,
    far_lists,
):
    basis = leaf_basis.reshape(PAIRS, 128, 128)
    transfer = leaf_transfer.reshape(PAIRS, 128, 64)
    coupling = leaf_coupling.reshape(LEAVES, 512, 64)
    win, cwin, pts, local = run_comm(
        coords, rhs, basis, transfer, upper_transfer[0], upper_coupling.reshape(16, 64, 64)
    )
    return run_field(
        near_lists.T, near_counts, far_lists.T, coupling, transfer, basis, rhs, win, cwin, pts, local
    )


def solution(mesh):
    return jax.shard_map(
        per_device,
        mesh=mesh,
        in_specs=(
            P(None, "leaf"),
            P(None, "leaf"),
            P("leaf", None, None),
            P("leaf", None, None),
            P("leaf", None, None, None),
            P("leaf", None, None, None, None),
            P("leaf", None, None, None),
            P("leaf", None),
            P("leaf"),
            P("leaf", None),
        ),
        out_specs=P(None, "leaf"),
        check_vma=False,
    )
```

```python
import functools
import math

import jax
import jax.numpy as jnp
from jax import lax
from jax.experimental import pallas as pl
from jax.experimental.pallas import tpu as pltpu
from jax.sharding import PartitionSpec as P

S_RATE = 3.0**0.5 / 0.2
C_RATE = S_RATE * math.log2(math.e)
NOISE = 0.1
OFFSETS = (-3, -2, 2, 3)
HALO = (-2, -1, 1, 2)
LEAVES = 40
PAIRS = LEAVES // 2
SLOTS = 27
LEVELS = 4
BATCH = 8
SIDE = 0
COEF_UNROLL = 10
HALO_CUT = 30
TINY = 1e-12
MESH = pl.DeviceIdType.MESH
bf16 = jnp.bfloat16
f32 = jnp.float32
NT = (((1,), (1,)), ((), ()))
TN = (((0,), (0,)), ((), ()))


def rounded(x):
    return x.astype(bf16).astype(f32)


def dot(a, b):
    return jnp.dot(a, b, preferred_element_type=f32)


def dot_nt(a, b):
    return lax.dot_general(a, b, NT, preferred_element_type=f32)


def norm_pieces(c):
    sq = c * c
    n2 = sq[0:1] + sq[1:2] + sq[2:3]
    high = rounded(n2)
    mid = rounded(n2 - high)
    low = n2 - high - mid
    return high, mid, low


def comm_kernel(
    coords_h,
    rhs_h,
    basis_h,
    transfer_h,
    up_t_h,
    up_c_h,
    win,
    cwin,
    pts_h,
    local_h,
    coords,
    rhs,
    basis,
    transfer,
    up_t,
    up_c,
    load_sems,
    own,
    cown,
    pts,
    local,
    blank,
    store_sems,
    blank_sems,
    tsend,
    trecv,
    lev,
    lrecv,
    halo_send,
    halo_recv,
    term_send,
    term_recv,
    lev_send,
    lev_recv,
):
    n = lax.axis_size("leaf")
    me = lax.axis_index("leaf")
    pairs = [
        (coords_h, coords),
        (rhs_h, rhs),
        (basis_h, basis),
        (transfer_h, transfer),
        (up_t_h, up_t),
        (up_c_h, up_c),
    ]
    loads = [pltpu.make_async_copy(a, b, load_sems.at[num]) for num, (a, b) in enumerate(pairs)]
    for load in loads:
        load.start()

    def away(k):
        return lax.rem(me + k + n, n)

    def partner(m):
        bits = [lax.rem(me, 2), lax.rem(me // 2, 2), lax.rem(me // 4, 2)]
        other = me
        for b in range(3):
            if m >> b & 1:
                other = other + (1 - 2 * bits[b]) * (1 << b)
        return other

    def inside(k):
        return jnp.logical_and(me + k >= 0, me + k < n)

    steps = sorted({2} | {abs(o) << j for j in range(LEVELS) for o in OFFSETS})
    steps = steps + [-k for k in steps]
    lrecv[...] = jnp.zeros_like(lrecv)
    barrier = pltpu.get_barrier_semaphore()
    for m in range(1, 8):
        pl.semaphore_signal(barrier, inc=1, device_id=(partner(m),), device_id_type=MESH)
    greeted = jnp.int32(7)
    for k in steps:
        greeted = greeted + jnp.where(inside(k), 1, 0)

        @pl.when(inside(k))
        def _(k=k):
            pl.semaphore_signal(barrier, inc=1, device_id=(away(k),), device_id_type=MESH)

    ones2 = jnp.ones((2, 128), f32)
    ones3 = jnp.ones((3, 128), f32)
    zero8 = jnp.zeros((8, 128), f32)

    def build(i, carry):
        at = pl.ds(pl.multiple_of(i * 128, 128), 128)
        c = coords[:, at].astype(f32)
        high, mid, low = norm_pieces(c)
        tile = jnp.concatenate([rhs[:, at], c, high, mid, low, ones2], axis=0)
        own[i] = tile.astype(bf16)
        return carry

    for load in loads[:2]:
        load.wait()
    lax.fori_loop(0, LEAVES, build, 0, unroll=4)

    lane = lax.broadcasted_iota(jnp.int32, (8, 128), 1)

    def coef_four(u, total):
        halves = []
        for h in range(2):
            t = 2 * u + h
            at = pl.ds(pl.multiple_of(t * 256, 256), 256)
            r = rhs[:, at]
            both = jnp.concatenate([r[:, :128], r[:, 128:]], axis=0).astype(bf16)
            x = dot_nt(both, basis[t])
            pair = jnp.where(lane < 64, x[:8], x[8:])
            halves.append(pair)
            total = total + dot(pair.astype(bf16), transfer[t])
        cown[u] = jnp.concatenate(halves, axis=0).astype(bf16)
        return total

    for load in loads[2:]:
        load.wait()
    level_zero = lax.fori_loop(0, PAIRS // 2, coef_four, jnp.zeros((8, 64), f32), unroll=COEF_UNROLL)
    zero64 = jnp.zeros((8, 64), f32)

    def widen(x):
        return jnp.concatenate([x, zero64], axis=1)

    half = level_zero.astype(bf16)
    lev[0] = widen(half.astype(f32))
    for j in range(3):
        tsend[2 - j] = widen(dot(half, up_t[j]))

    blank[...] = jnp.zeros_like(blank)
    stores = [
        pltpu.make_async_copy(own, win.at[pl.ds(2 * LEAVES, LEAVES)], store_sems.at[0]),
        pltpu.make_async_copy(cown, cwin.at[pl.ds(PAIRS, PAIRS // 2)], store_sems.at[1]),
    ]
    for store in stores:
        store.start()

    def clears(num, k):
        return (
            pltpu.make_async_copy(
                blank, win.at[pl.ds((2 + k) * LEAVES, LEAVES)], blank_sems.at[num, 0]
            ),
            pltpu.make_async_copy(
                blank.at[pl.ds(0, PAIRS // 2)],
                cwin.at[pl.ds((2 + k) * (PAIRS // 2), PAIRS // 2)],
                blank_sems.at[num, 1],
            ),
        )

    for num, k in enumerate(HALO):
        @pl.when(jnp.logical_not(inside(k)))
        def _(num=num, k=k):
            for clear in clears(num, k):
                clear.start()

    pl.semaphore_wait(barrier, greeted)

    terms = []
    for m in range(1, 8):
        count = 3 if m == 1 else 2 if m < 4 else 1
        terms.append(
            pltpu.make_async_remote_copy(
                src_ref=tsend.at[pl.ds(0, count)],
                dst_ref=trecv.at[m, pl.ds(0, count)],
                send_sem=term_send.at[m],
                recv_sem=term_recv.at[m],
                device_id=(partner(m),),
                device_id_type=MESH,
            )
        )
        terms[-1].start()

    copies = []

    def begin(k, copy):
        copies.append((k, copy))

        @pl.when(inside(k))
        def _():
            copy.start()

    def finish(some):
        for k, copy in some:
            @pl.when(inside(k))
            def _(copy=copy):
                copy.wait_send()

            @pl.when(inside(-k))
            def _(copy=copy):
                copy.wait_recv()

    def send_level(j):
        for num, o in enumerate(OFFSETS):
            k = -o * 2**j
            copy = pltpu.make_async_remote_copy(
                src_ref=lev.at[j],
                dst_ref=lrecv.at[j, num],
                send_sem=lev_send.at[j, num],
                recv_sem=lev_recv.at[j, num],
                device_id=(away(k),),
                device_id_type=MESH,
            )
            begin(k, copy)

    send_level(0)
    core = lax.rem(me, 2)
    sibling = me + 1 - 2 * core
    chunks = [
        (own, win, LEAVES, 0, HALO_CUT),
        (own, win, LEAVES, HALO_CUT, LEAVES - HALO_CUT),
        (cown, cwin, PAIRS // 2, 0, PAIRS // 2),
    ]

    def halo_copy(route, part, src, slot, device):
        _, ref, rows, at, size = chunks[part]
        return pltpu.make_async_remote_copy(
            src_ref=src,
            dst_ref=ref.at[pl.ds(slot * rows + at, size)],
            send_sem=halo_send.at[route, part],
            recv_sem=halo_recv.at[route, part],
            device_id=(device,),
            device_id_type=MESH,
        )

    outer = {}
    to_sibling = []

    def send_halo(part):
        mine, _, _, at, size = chunks[part]
        src = mine.at[pl.ds(at, size)]
        for route, k in enumerate((-2, 2)):
            copy = halo_copy(route, part, src, 2 - k, away(k))
            outer[k, part] = copy

            @pl.when(inside(k))
            def _(copy=copy):
                copy.start()

        to_sibling.append(halo_copy(2, part, src, 1 + 2 * core, sibling))
        to_sibling[-1].start()

    send_halo(2)
    send_halo(0)

    for copy in terms:
        copy.wait()
    for j in (1, 2, 3):
        total = tsend[3 - j]
        for m in range(1, 2**j):
            total = total + trecv[m, 3 - j]
        lev[j] = rounded(total)
        send_level(j)

    send_halo(1)

    def build_points(i, carry):
        at = pl.ds(pl.multiple_of(i * 128, 128), 128)
        c = coords[:, at].astype(f32)
        high, mid, low = norm_pieces(c)
        tile = jnp.concatenate([zero8, -2.0 * c, ones3, high, mid], axis=0)
        pts[i] = tile.T.astype(bf16)
        return carry

    lax.fori_loop(0, LEAVES, build_points, 0, unroll=4)
    stores.append(pltpu.make_async_copy(pts, pts_h, store_sems.at[2]))
    stores[-1].start()

    forwards = {}

    def forward_halo(part):
        _, ref, rows, at, size = chunks[part]
        src = ref.at[pl.ds((4 - 4 * core) * rows + at, size)]
        copy = halo_copy(3, part, src, 3 - 2 * core, sibling)
        forwards[part] = copy

        @pl.when(jnp.logical_and(core == 0, inside(2)))
        def _():
            outer[-2, part].wait_recv()
            copy.start()

        @pl.when(jnp.logical_and(core == 1, inside(-2)))
        def _():
            outer[2, part].wait_recv()
            copy.start()

    forward_halo(2)
    forward_halo(0)
    forward_halo(1)
    finish(copies)
    total = jnp.zeros((8, 64), f32)
    for j in range(LEVELS):
        for num in range(4):
            coef = lrecv[j, num][:, :64]
            total = total + dot(coef.astype(bf16), up_c[4 * j + num])
    local[...] = total
    stores.append(pltpu.make_async_copy(local, local_h, store_sems.at[3]))
    stores[-1].start()
    for store in stores:
        store.wait()
    for num, k in enumerate(HALO):
        @pl.when(jnp.logical_not(inside(k)))
        def _(num=num, k=k):
            for clear in clears(num, k):
                clear.wait()

    for copy in to_sibling:
        copy.wait()
    for part in range(3):
        for k in (-2, 2):
            @pl.when(inside(k))
            def _(copy=outer[k, part]):
                copy.wait_send()

        @pl.when(jnp.logical_and(core == 1, inside(2)))
        def _(copy=outer[-2, part]):
            copy.wait_recv()

        @pl.when(jnp.logical_and(core == 0, inside(-2)))
        def _(copy=outer[2, part]):
            copy.wait_recv()

        @pl.when(inside(2 - 4 * core))
        def _(copy=forwards[part]):
            copy.wait_send()

        @pl.when(inside(2 * core - 1))
        def _(copy=forwards[part]):
            copy.wait_recv()


def matern(u):
    u = jnp.maximum(u, TINY)
    r = u * lax.rsqrt(u)
    return ((1.0 + S_RATE * r) * jnp.exp2(-C_RATE * r)).astype(bf16)


def expand_coefs(cwin, table, first):
    def expand(t, carry):
        x = cwin[t].astype(f32)
        y = pltpu.roll(x, 64, 1)
        for h in range(2):
            a, b = x[8 * h : 8 * h + 8], y[8 * h : 8 * h + 8]
            table[4 * t + 2 * h] = jnp.where(first, a, b)
            table[4 * t + 2 * h + 1] = jnp.where(first, b, a)
        return carry

    lax.fori_loop(0, 5 * PAIRS // 2, expand, 0, unroll=5)


def far_stage(fars, cwin, local, coupling, transfer, basis, rhs, out, table, held):
    first = lax.broadcasted_iota(jnp.int32, (8, 128), 1) < 64
    expand_coefs(cwin, table, first)
    local_half = local[...].astype(bf16)

    def far_sums(t):
        sums = []
        for h in range(2):
            i = 2 * t + h
            cols = [
                jnp.where(first, table[fars[2 * m, i]], table[fars[2 * m + 1, i]]) for m in range(4)
            ]
            x = jnp.concatenate(cols, axis=1).astype(bf16)
            sums.append(dot(x, coupling[i]))
        both = jnp.concatenate(sums, axis=1) + dot_nt(local_half, transfer[t])
        held[...] = rounded(both)

    def far_field(t):
        both = held[...]
        zero = jnp.zeros_like(both)
        split = jnp.concatenate([jnp.where(first, both, zero), jnp.where(first, zero, both)], axis=0)
        far = dot(split.astype(bf16), basis[t])
        for h in range(2):
            at = pl.ds(pl.multiple_of(t * 256 + h * 128, 128), 128)
            out[:, at] += far[8 * h : 8 * h + 8] + NOISE * rhs[:, at]

    return far_sums, far_field


def field_phase(lists, counts, win, pts, out, dist, block, prepare_far):
    out[...] = jnp.zeros_like(out)
    nothing = jnp.zeros((16, 128), bf16)

    def advance(leaf, s):
        n = counts[jnp.minimum(leaf, LEAVES - 1)]
        last = s + 2 >= n
        return jnp.where(last, leaf + 1, leaf), jnp.where(last, 0, s + 2)

    def batch_from(leaf, s):
        batch = []
        for _ in range(BATCH):
            batch.append((leaf, s))
            leaf, s = advance(leaf, s)
        return batch, leaf, s

    def entries(leaf, s):
        i = jnp.minimum(leaf, LEAVES - 1)
        return i, lists[s, i], lists[jnp.minimum(s + 1, SLOTS - 1), i]

    def distance(leaf, s, g):
        i, a, b = entries(leaf, s)
        q = jnp.concatenate([win[a], win[b]], axis=1 - SIDE)
        if SIDE:
            dist[g] = lax.dot_general(q, pts[i], TN, preferred_element_type=f32)
        else:
            dist[g] = dot(pts[i], q)

    def values(g):
        block[g] = matern(dist[g])

    def product(leaf, s, g):
        i, a, b = entries(leaf, s)
        live = leaf < LEAVES
        both = jnp.logical_and(live, s + 1 < counts[i])
        ra = jnp.where(live, win[a], nothing)
        rb = jnp.where(both, win[b], nothing)
        r = jnp.concatenate([ra, rb], axis=1)
        k = block[g]
        if SIDE:
            d = dot(r, jnp.concatenate([k[:, :128], k[:, 128:]], axis=0))
        else:
            d = dot_nt(r, k)
        at = pl.ds(pl.multiple_of(i * 128, 128), 128)
        out[:, at] += d[:8]

    tasks = lax.fori_loop(0, LEAVES, lambda i, t: t + (counts[i] + 1) // 2, jnp.int32(0))
    zero = jnp.int32(0)
    now, leaf, s = batch_from(zero, zero)
    for g in range(BATCH):
        distance(*now[g], g)
    mid, leaf, s = batch_from(leaf, s)
    for g in range(BATCH):
        values(g)
        distance(*mid[g], g)

    def near_step(carry, extra=None):
        now, mid, leaf, s = carry
        later, leaf, s = batch_from(leaf, s)
        for g in range(BATCH):
            if extra and g in extra:
                extra[g]()
            product(*now[g], g)
            values(g)
            distance(*later[g], g)
        return mid, later, leaf, s

    rounds = (tasks + BATCH - 1) // BATCH
    shared = jnp.minimum(rounds, PAIRS)
    carry = lax.fori_loop(0, rounds - shared, lambda _, c: near_step(c), (now, mid, leaf, s))
    far_sums, far_field = prepare_far()

    def both_steps(t, carry):
        return near_step(carry, {1: lambda: far_sums(t), 7: lambda: far_field(t)})

    def far_step(t, carry):
        far_sums(t)
        far_field(t)
        return carry

    lax.fori_loop(0, shared, both_steps, carry)
    lax.fori_loop(shared, PAIRS, far_step, 0)


def field_kernel(
    lists_h,
    counts_h,
    fars_h,
    coupling_h,
    transfer_h,
    basis_h,
    rhs_h,
    win_h,
    cwin_h,
    pts_h,
    local_h,
    out,
    lists,
    counts,
    fars,
    coupling,
    transfer,
    basis,
    rhs,
    win,
    cwin,
    pts,
    local,
    sems,
    table,
    held,
    dist,
    block,
):
    pairs = [
        (lists_h, lists),
        (counts_h, counts),
        (win_h, win),
        (pts_h, pts),
        (fars_h, fars),
        (cwin_h, cwin),
        (local_h, local),
        (coupling_h, coupling),
        (transfer_h, transfer),
        (basis_h, basis),
        (rhs_h, rhs),
    ]
    copies = [pltpu.make_async_copy(a, b, sems.at[n]) for n, (a, b) in enumerate(pairs)]
    for copy in copies[:4]:
        copy.start()
    for copy in copies[:4]:
        copy.wait()
    for copy in copies[4:]:
        copy.start()
    def prepare_far():
        for copy in copies[4:]:
            copy.wait()
        return far_stage(fars, cwin, local, coupling, transfer, basis, rhs, out, table, held)

    field_phase(lists, counts, win, pts, out, dist, block, prepare_far)


def run_field(lists, counts, fars, coupling, transfer, basis, rhs, *arrays):
    hbm = pl.BlockSpec(memory_space=pltpu.HBM)
    vmem = pl.BlockSpec(memory_space=pltpu.VMEM)
    return pl.pallas_call(
        field_kernel,
        out_shape=jax.ShapeDtypeStruct((8, LEAVES * 128), f32),
        in_specs=[hbm] * (7 + len(arrays)),
        out_specs=vmem,
        scratch_shapes=[
            pltpu.SMEM((SLOTS, LEAVES), jnp.int32),
            pltpu.SMEM((LEAVES,), jnp.int32),
            pltpu.SMEM((8, LEAVES), jnp.int32),
            pltpu.VMEM((LEAVES, 512, 64), bf16),
            pltpu.VMEM((PAIRS, 128, 64), bf16),
            pltpu.VMEM((PAIRS, 128, 128), bf16),
            pltpu.VMEM((8, LEAVES * 128), f32),
            *[pltpu.VMEM(x.shape, x.dtype) for x in arrays],
            pltpu.SemaphoreType.DMA((11,)),
            pltpu.VMEM((5 * LEAVES, 8, 128), f32),
            pltpu.VMEM((8, 128), f32),
            pltpu.VMEM((BATCH, 128, 256), f32),
            pltpu.VMEM((BATCH, 128, 256), bf16),
        ],
        compiler_params=pltpu.CompilerParams(vmem_limit_bytes=60 * 2**20),
    )(lists, counts, fars, coupling, transfer, basis, rhs, *arrays)


def run_comm(*arrays):
    hbm = pl.BlockSpec(memory_space=pltpu.HBM)
    dma = pltpu.SemaphoreType.DMA
    return pl.pallas_call(
        comm_kernel,
        out_shape=[
            jax.ShapeDtypeStruct((5 * LEAVES, 16, 128), bf16),
            jax.ShapeDtypeStruct((5 * PAIRS // 2, 16, 128), bf16),
            jax.ShapeDtypeStruct((LEAVES, 128, 16), bf16),
            jax.ShapeDtypeStruct((8, 64), f32),
        ],
        in_specs=[hbm] * len(arrays),
        out_specs=[hbm] * 4,
        scratch_shapes=[pltpu.VMEM(x.shape, x.dtype) for x in arrays]
        + [
            dma((6,)),
            pltpu.VMEM((LEAVES, 16, 128), bf16),
            pltpu.VMEM((PAIRS // 2, 16, 128), bf16),
            pltpu.VMEM((LEAVES, 128, 16), bf16),
            pltpu.VMEM((8, 64), f32),
            pltpu.VMEM((LEAVES, 16, 128), bf16),
            dma((4,)),
            dma((4, 2)),
            pltpu.VMEM((3, 8, 128), f32),
            pltpu.VMEM((8, 3, 8, 128), f32),
            pltpu.VMEM((LEVELS, 8, 128), f32),
            pltpu.VMEM((LEVELS, 4, 8, 128), f32),
            dma((4, 3)),
            dma((4, 3)),
            dma((8,)),
            dma((8,)),
            dma((LEVELS, 4)),
            dma((LEVELS, 4)),
        ],
        compiler_params=pltpu.CompilerParams(
            collective_id=0, has_side_effects=True, vmem_limit_bytes=60 * 2**20
        ),
    )(*arrays)


def per_device(
    coords,
    rhs,
    leaf_basis,
    leaf_transfer,
    upper_transfer,
    upper_coupling,
    leaf_coupling,
    near_lists,
    near_counts,
    far_lists,
):
    basis = leaf_basis.reshape(PAIRS, 128, 128)
    transfer = leaf_transfer.reshape(PAIRS, 128, 64)
    coupling = leaf_coupling.reshape(LEAVES, 512, 64)
    win, cwin, pts, local = run_comm(
        coords, rhs, basis, transfer, upper_transfer[0], upper_coupling.reshape(16, 64, 64)
    )
    return run_field(
        near_lists.T, near_counts, far_lists.T, coupling, transfer, basis, rhs, win, cwin, pts, local
    )


def solution(mesh):
    return jax.shard_map(
        per_device,
        mesh=mesh,
        in_specs=(
            P(None, "leaf"),
            P(None, "leaf"),
            P("leaf", None, None),
            P("leaf", None, None),
            P("leaf", None, None, None),
            P("leaf", None, None, None, None),
            P("leaf", None, None, None),
            P("leaf", None),
            P("leaf"),
            P("leaf", None),
        ),
        out_specs=P(None, "leaf"),
        check_vma=False,
    )
```

```python
import functools
import math

import jax
import jax.numpy as jnp
from jax import lax
from jax.experimental import pallas as pl
from jax.experimental.pallas import tpu as pltpu
from jax.sharding import PartitionSpec as P

LOG2_E = math.log2(math.e)
SQ_RATE = 75.0
NOISE = 0.1
OFFSETS = (-3, -2, 2, 3)
HALO = (-2, -1, 1, 2)
LEAVES = 40
PAIRS = LEAVES // 2
SLOTS = 27
LEVELS = 4
BATCH = 8
COEF_UNROLL = 10
HALO_CUT = 30
TINY = 1e-12
MESH = pl.DeviceIdType.MESH
bf16 = jnp.bfloat16
f32 = jnp.float32
NT = (((1,), (1,)), ((), ()))


def rounded(x):
    return x.astype(bf16).astype(f32)


def dot(a, b):
    return jnp.dot(a, b, preferred_element_type=f32)


def dot_nt(a, b):
    return lax.dot_general(a, b, NT, preferred_element_type=f32)


def norm_pieces(c):
    sq = c * c
    n2 = SQ_RATE * (sq[0:1] + sq[1:2] + sq[2:3])
    high = rounded(n2)
    mid = rounded(n2 - high)
    low = n2 - high - mid
    return high, mid, low


def comm_kernel(
    coords_h,
    rhs_h,
    basis_h,
    transfer_h,
    up_t_h,
    up_c_h,
    win,
    cwin,
    pts_h,
    local_h,
    coords,
    rhs,
    basis,
    transfer,
    up_t,
    up_c,
    load_sems,
    own,
    cown,
    pts,
    local,
    blank,
    store_sems,
    blank_sems,
    tsend,
    trecv,
    lev,
    lrecv,
    halo_send,
    halo_recv,
    term_send,
    term_recv,
    lev_send,
    lev_recv,
):
    n = lax.axis_size("leaf")
    me = lax.axis_index("leaf")
    pairs = [
        (coords_h, coords),
        (rhs_h, rhs),
        (basis_h, basis),
        (transfer_h, transfer),
        (up_t_h, up_t),
        (up_c_h, up_c),
    ]
    loads = [pltpu.make_async_copy(a, b, load_sems.at[num]) for num, (a, b) in enumerate(pairs)]
    for load in loads:
        load.start()

    def away(k):
        return lax.rem(me + k + n, n)

    def partner(m):
        bits = [lax.rem(me, 2), lax.rem(me // 2, 2), lax.rem(me // 4, 2)]
        other = me
        for b in range(3):
            if m >> b & 1:
                other = other + (1 - 2 * bits[b]) * (1 << b)
        return other

    def inside(k):
        return jnp.logical_and(me + k >= 0, me + k < n)

    steps = sorted({2} | {abs(o) << j for j in range(LEVELS) for o in OFFSETS})
    steps = steps + [-k for k in steps]
    lrecv[...] = jnp.zeros_like(lrecv)
    barrier = pltpu.get_barrier_semaphore()
    for m in range(1, 8):
        pl.semaphore_signal(barrier, inc=1, device_id=(partner(m),), device_id_type=MESH)
    greeted = jnp.int32(7)
    for k in steps:
        greeted = greeted + jnp.where(inside(k), 1, 0)

        @pl.when(inside(k))
        def _(k=k):
            pl.semaphore_signal(barrier, inc=1, device_id=(away(k),), device_id_type=MESH)

    ones2 = jnp.ones((2, 128), f32)
    ones3 = jnp.ones((3, 128), f32)
    zero8 = jnp.zeros((8, 128), f32)
    zero3 = jnp.zeros((3, 128), f32)
    zero1 = jnp.zeros((1, 128), f32)

    def build(i, carry):
        at = pl.ds(pl.multiple_of(i * 128, 128), 128)
        c = coords[:, at].astype(f32)
        high, mid, low = norm_pieces(c)
        tile = jnp.concatenate([rhs[:, at], c, high, mid, low, ones2], axis=0)
        own[i] = tile.astype(bf16)
        return carry

    for load in loads[:2]:
        load.wait()
    lax.fori_loop(0, LEAVES, build, 0, unroll=4)

    lane = lax.broadcasted_iota(jnp.int32, (8, 128), 1)

    def coef_four(u, total):
        halves = []
        for h in range(2):
            t = 2 * u + h
            at = pl.ds(pl.multiple_of(t * 256, 256), 256)
            r = rhs[:, at]
            both = jnp.concatenate([r[:, :128], r[:, 128:]], axis=0).astype(bf16)
            x = dot_nt(both, basis[t])
            pair = jnp.where(lane < 64, x[:8], x[8:])
            halves.append(pair)
            total = total + dot(pair.astype(bf16), transfer[t])
        cown[u] = jnp.concatenate(halves, axis=0).astype(bf16)
        return total

    for load in loads[2:]:
        load.wait()
    level_zero = lax.fori_loop(0, PAIRS // 2, coef_four, jnp.zeros((8, 64), f32), unroll=COEF_UNROLL)
    zero64 = jnp.zeros((8, 64), f32)

    def widen(x):
        return jnp.concatenate([x, zero64], axis=1)

    half = level_zero.astype(bf16)
    lev[0] = widen(half.astype(f32))
    for j in range(3):
        tsend[2 - j] = widen(dot(half, up_t[j]))

    blank[...] = jnp.zeros_like(blank)
    stores = [
        pltpu.make_async_copy(own, win.at[pl.ds(2 * LEAVES, LEAVES)], store_sems.at[0]),
        pltpu.make_async_copy(cown, cwin.at[pl.ds(PAIRS, PAIRS // 2)], store_sems.at[1]),
    ]
    for store in stores:
        store.start()

    def clears(num, k):
        return (
            pltpu.make_async_copy(
                blank, win.at[pl.ds((2 + k) * LEAVES, LEAVES)], blank_sems.at[num, 0]
            ),
            pltpu.make_async_copy(
                blank.at[pl.ds(0, PAIRS // 2)],
                cwin.at[pl.ds((2 + k) * (PAIRS // 2), PAIRS // 2)],
                blank_sems.at[num, 1],
            ),
        )

    for num, k in enumerate(HALO):
        @pl.when(jnp.logical_not(inside(k)))
        def _(num=num, k=k):
            for clear in clears(num, k):
                clear.start()

    pl.semaphore_wait(barrier, greeted)

    terms = []
    for m in range(1, 8):
        count = 3 if m == 1 else 2 if m < 4 else 1
        terms.append(
            pltpu.make_async_remote_copy(
                src_ref=tsend.at[pl.ds(0, count)],
                dst_ref=trecv.at[m, pl.ds(0, count)],
                send_sem=term_send.at[m],
                recv_sem=term_recv.at[m],
                device_id=(partner(m),),
                device_id_type=MESH,
            )
        )
        terms[-1].start()

    copies = []

    def begin(k, copy):
        copies.append((k, copy))

        @pl.when(inside(k))
        def _():
            copy.start()

    def finish(some):
        for k, copy in some:
            @pl.when(inside(k))
            def _(copy=copy):
                copy.wait_send()

            @pl.when(inside(-k))
            def _(copy=copy):
                copy.wait_recv()

    def send_level(j):
        for num, o in enumerate(OFFSETS):
            k = -o * 2**j
            copy = pltpu.make_async_remote_copy(
                src_ref=lev.at[j],
                dst_ref=lrecv.at[j, num],
                send_sem=lev_send.at[j, num],
                recv_sem=lev_recv.at[j, num],
                device_id=(away(k),),
                device_id_type=MESH,
            )
            begin(k, copy)

    send_level(0)
    core = lax.rem(me, 2)
    sibling = me + 1 - 2 * core
    chunks = [
        (own, win, LEAVES, 0, HALO_CUT),
        (own, win, LEAVES, HALO_CUT, LEAVES - HALO_CUT),
        (cown, cwin, PAIRS // 2, 0, PAIRS // 2),
    ]

    def halo_copy(route, part, src, slot, device):
        _, ref, rows, at, size = chunks[part]
        return pltpu.make_async_remote_copy(
            src_ref=src,
            dst_ref=ref.at[pl.ds(slot * rows + at, size)],
            send_sem=halo_send.at[route, part],
            recv_sem=halo_recv.at[route, part],
            device_id=(device,),
            device_id_type=MESH,
        )

    outer = {}
    to_sibling = []

    def send_halo(part):
        mine, _, _, at, size = chunks[part]
        src = mine.at[pl.ds(at, size)]
        for route, k in enumerate((-2, 2)):
            copy = halo_copy(route, part, src, 2 - k, away(k))
            outer[k, part] = copy

            @pl.when(inside(k))
            def _(copy=copy):
                copy.start()

        to_sibling.append(halo_copy(2, part, src, 1 + 2 * core, sibling))
        to_sibling[-1].start()

    send_halo(2)
    send_halo(0)

    for copy in terms:
        copy.wait()
    for j in (1, 2, 3):
        total = tsend[3 - j]
        for m in range(1, 2**j):
            total = total + trecv[m, 3 - j]
        lev[j] = rounded(total)
        send_level(j)

    send_halo(1)

    def build_points(i, carry):
        at = pl.ds(pl.multiple_of(i * 128, 128), 128)
        c = coords[:, at].astype(f32)
        high, mid, low = norm_pieces(c)
        whole = (-2.0 * SQ_RATE) * c
        main = rounded(whole)
        rows = [zero8, main, ones3, high, mid, zero8, whole - main, zero3, low, zero1]
        tile = jnp.concatenate(rows, axis=0)
        pts[i] = tile.T.astype(bf16)
        return carry

    lax.fori_loop(0, LEAVES, build_points, 0, unroll=4)
    stores.append(pltpu.make_async_copy(pts, pts_h, store_sems.at[2]))
    stores[-1].start()

    forwards = {}

    def forward_halo(part):
        _, ref, rows, at, size = chunks[part]
        src = ref.at[pl.ds((4 - 4 * core) * rows + at, size)]
        copy = halo_copy(3, part, src, 3 - 2 * core, sibling)
        forwards[part] = copy

        @pl.when(jnp.logical_and(core == 0, inside(2)))
        def _():
            outer[-2, part].wait_recv()
            copy.start()

        @pl.when(jnp.logical_and(core == 1, inside(-2)))
        def _():
            outer[2, part].wait_recv()
            copy.start()

    forward_halo(2)
    forward_halo(0)
    forward_halo(1)
    finish(copies)
    total = jnp.zeros((8, 64), f32)
    for j in range(LEVELS):
        for num in range(4):
            coef = lrecv[j, num][:, :64]
            total = total + dot(coef.astype(bf16), up_c[4 * j + num])
    local[...] = total
    stores.append(pltpu.make_async_copy(local, local_h, store_sems.at[3]))
    stores[-1].start()
    for store in stores:
        store.wait()
    for num, k in enumerate(HALO):
        @pl.when(jnp.logical_not(inside(k)))
        def _(num=num, k=k):
            for clear in clears(num, k):
                clear.wait()

    for copy in to_sibling:
        copy.wait()
    for part in range(3):
        for k in (-2, 2):
            @pl.when(inside(k))
            def _(copy=outer[k, part]):
                copy.wait_send()

        @pl.when(jnp.logical_and(core == 1, inside(2)))
        def _(copy=outer[-2, part]):
            copy.wait_recv()

        @pl.when(jnp.logical_and(core == 0, inside(-2)))
        def _(copy=outer[2, part]):
            copy.wait_recv()

        @pl.when(inside(2 - 4 * core))
        def _(copy=forwards[part]):
            copy.wait_send()

        @pl.when(inside(2 * core - 1))
        def _(copy=forwards[part]):
            copy.wait_recv()


def matern(u):
    u = jnp.maximum(u, TINY)
    x = u * lax.rsqrt(u)
    return ((1.0 + x) * jnp.exp2(-LOG2_E * x)).astype(bf16)


def expand_coefs(cwin, table, first):
    def expand(t, carry):
        x = cwin[t].astype(f32)
        y = pltpu.roll(x, 64, 1)
        for h in range(2):
            a, b = x[8 * h : 8 * h + 8], y[8 * h : 8 * h + 8]
            table[4 * t + 2 * h] = jnp.where(first, a, b)
            table[4 * t + 2 * h + 1] = jnp.where(first, b, a)
        return carry

    lax.fori_loop(0, 5 * PAIRS // 2, expand, 0, unroll=5)


def far_stage(fars, cwin, local, coupling, transfer, basis, rhs, out, table, held):
    first = lax.broadcasted_iota(jnp.int32, (8, 128), 1) < 64
    expand_coefs(cwin, table, first)
    local_half = local[...].astype(bf16)

    def far_sums(t):
        sums = []
        for h in range(2):
            i = 2 * t + h
            cols = [
                jnp.where(first, table[fars[2 * m, i]], table[fars[2 * m + 1, i]]) for m in range(4)
            ]
            x = jnp.concatenate(cols, axis=1).astype(bf16)
            sums.append(dot(x, coupling[i]))
        both = jnp.concatenate(sums, axis=1) + dot_nt(local_half, transfer[t])
        held[...] = rounded(both)

    def far_field(t):
        both = held[...]
        zero = jnp.zeros_like(both)
        split = jnp.concatenate([jnp.where(first, both, zero), jnp.where(first, zero, both)], axis=0)
        far = dot(split.astype(bf16), basis[t])
        for h in range(2):
            at = pl.ds(pl.multiple_of(t * 256 + h * 128, 128), 128)
            out[:, at] += far[8 * h : 8 * h + 8] + NOISE * rhs[:, at]

    return far_sums, far_field


def field_phase(lists, counts, win, pts, out, dist, block, prepare_far):
    out[...] = jnp.zeros_like(out)
    nothing = jnp.zeros((16, 128), bf16)

    def advance(leaf, s):
        n = counts[jnp.minimum(leaf, LEAVES - 1)]
        last = s + 2 >= n
        return jnp.where(last, leaf + 1, leaf), jnp.where(last, 0, s + 2)

    def batch_from(leaf, s):
        batch = []
        for _ in range(BATCH):
            batch.append((leaf, s))
            leaf, s = advance(leaf, s)
        return batch, leaf, s

    def entries(leaf, s):
        i = jnp.minimum(leaf, LEAVES - 1)
        return i, lists[s, i], lists[jnp.minimum(s + 1, SLOTS - 1), i]

    def distance(leaf, s, g):
        i, a, b = entries(leaf, s)
        q = jnp.concatenate([win[a], win[b]], axis=1)
        dist[g] = dot(pts[i], jnp.concatenate([q, q], axis=0))

    def values(g):
        block[g] = matern(dist[g])

    def product(leaf, s, g):
        i, a, b = entries(leaf, s)
        live = leaf < LEAVES
        both = jnp.logical_and(live, s + 1 < counts[i])
        ra = jnp.where(live, win[a], nothing)
        rb = jnp.where(both, win[b], nothing)
        r = jnp.concatenate([ra, rb], axis=1)
        k = block[g]
        d = dot_nt(r, k)
        at = pl.ds(pl.multiple_of(i * 128, 128), 128)
        out[:, at] += d[:8]

    tasks = lax.fori_loop(0, LEAVES, lambda i, t: t + (counts[i] + 1) // 2, jnp.int32(0))
    zero = jnp.int32(0)
    now, leaf, s = batch_from(zero, zero)
    for g in range(BATCH):
        distance(*now[g], g)
    mid, leaf, s = batch_from(leaf, s)
    for g in range(BATCH):
        values(g)
        distance(*mid[g], g)

    def near_step(carry, extra=None):
        now, mid, leaf, s = carry
        later, leaf, s = batch_from(leaf, s)
        for g in range(BATCH):
            if extra and g in extra:
                extra[g]()
            product(*now[g], g)
            values(g)
            distance(*later[g], g)
        return mid, later, leaf, s

    rounds = (tasks + BATCH - 1) // BATCH
    shared = jnp.minimum(rounds, PAIRS)
    carry = lax.fori_loop(0, rounds - shared, lambda _, c: near_step(c), (now, mid, leaf, s))
    far_sums, far_field = prepare_far()

    def both_steps(t, carry):
        return near_step(carry, {1: lambda: far_sums(t), 7: lambda: far_field(t)})

    def far_step(t, carry):
        far_sums(t)
        far_field(t)
        return carry

    lax.fori_loop(0, shared, both_steps, carry)
    lax.fori_loop(shared, PAIRS, far_step, 0)


def field_kernel(
    lists_h,
    counts_h,
    fars_h,
    coupling_h,
    transfer_h,
    basis_h,
    rhs_h,
    win_h,
    cwin_h,
    pts_h,
    local_h,
    out,
    lists,
    counts,
    fars,
    coupling,
    transfer,
    basis,
    rhs,
    win,
    cwin,
    pts,
    local,
    sems,
    table,
    held,
    dist,
    block,
):
    pairs = [
        (lists_h, lists),
        (counts_h, counts),
        (win_h, win),
        (pts_h, pts),
        (fars_h, fars),
        (cwin_h, cwin),
        (local_h, local),
        (coupling_h, coupling),
        (transfer_h, transfer),
        (basis_h, basis),
        (rhs_h, rhs),
    ]
    copies = [pltpu.make_async_copy(a, b, sems.at[n]) for n, (a, b) in enumerate(pairs)]
    for copy in copies[:4]:
        copy.start()
    for copy in copies[:4]:
        copy.wait()
    for copy in copies[4:]:
        copy.start()
    def prepare_far():
        for copy in copies[4:]:
            copy.wait()
        return far_stage(fars, cwin, local, coupling, transfer, basis, rhs, out, table, held)

    field_phase(lists, counts, win, pts, out, dist, block, prepare_far)


def run_field(lists, counts, fars, coupling, transfer, basis, rhs, *arrays):
    hbm = pl.BlockSpec(memory_space=pltpu.HBM)
    vmem = pl.BlockSpec(memory_space=pltpu.VMEM)
    return pl.pallas_call(
        field_kernel,
        out_shape=jax.ShapeDtypeStruct((8, LEAVES * 128), f32),
        in_specs=[hbm] * (7 + len(arrays)),
        out_specs=vmem,
        scratch_shapes=[
            pltpu.SMEM((SLOTS, LEAVES), jnp.int32),
            pltpu.SMEM((LEAVES,), jnp.int32),
            pltpu.SMEM((8, LEAVES), jnp.int32),
            pltpu.VMEM((LEAVES, 512, 64), bf16),
            pltpu.VMEM((PAIRS, 128, 64), bf16),
            pltpu.VMEM((PAIRS, 128, 128), bf16),
            pltpu.VMEM((8, LEAVES * 128), f32),
            *[pltpu.VMEM(x.shape, x.dtype) for x in arrays],
            pltpu.SemaphoreType.DMA((11,)),
            pltpu.VMEM((5 * LEAVES, 8, 128), f32),
            pltpu.VMEM((8, 128), f32),
            pltpu.VMEM((BATCH, 128, 256), f32),
            pltpu.VMEM((BATCH, 128, 256), bf16),
        ],
        compiler_params=pltpu.CompilerParams(vmem_limit_bytes=60 * 2**20),
    )(lists, counts, fars, coupling, transfer, basis, rhs, *arrays)


def run_comm(*arrays):
    hbm = pl.BlockSpec(memory_space=pltpu.HBM)
    dma = pltpu.SemaphoreType.DMA
    return pl.pallas_call(
        comm_kernel,
        out_shape=[
            jax.ShapeDtypeStruct((5 * LEAVES, 16, 128), bf16),
            jax.ShapeDtypeStruct((5 * PAIRS // 2, 16, 128), bf16),
            jax.ShapeDtypeStruct((LEAVES, 128, 32), bf16),
            jax.ShapeDtypeStruct((8, 64), f32),
        ],
        in_specs=[hbm] * len(arrays),
        out_specs=[hbm] * 4,
        scratch_shapes=[pltpu.VMEM(x.shape, x.dtype) for x in arrays]
        + [
            dma((6,)),
            pltpu.VMEM((LEAVES, 16, 128), bf16),
            pltpu.VMEM((PAIRS // 2, 16, 128), bf16),
            pltpu.VMEM((LEAVES, 128, 32), bf16),
            pltpu.VMEM((8, 64), f32),
            pltpu.VMEM((LEAVES, 16, 128), bf16),
            dma((4,)),
            dma((4, 2)),
            pltpu.VMEM((3, 8, 128), f32),
            pltpu.VMEM((8, 3, 8, 128), f32),
            pltpu.VMEM((LEVELS, 8, 128), f32),
            pltpu.VMEM((LEVELS, 4, 8, 128), f32),
            dma((4, 3)),
            dma((4, 3)),
            dma((8,)),
            dma((8,)),
            dma((LEVELS, 4)),
            dma((LEVELS, 4)),
        ],
        compiler_params=pltpu.CompilerParams(
            collective_id=0, has_side_effects=True, vmem_limit_bytes=60 * 2**20
        ),
    )(*arrays)


def per_device(
    coords,
    rhs,
    leaf_basis,
    leaf_transfer,
    upper_transfer,
    upper_coupling,
    leaf_coupling,
    near_lists,
    near_counts,
    far_lists,
):
    basis = leaf_basis.reshape(PAIRS, 128, 128)
    transfer = leaf_transfer.reshape(PAIRS, 128, 64)
    coupling = leaf_coupling.reshape(LEAVES, 512, 64)
    win, cwin, pts, local = run_comm(
        coords, rhs, basis, transfer, upper_transfer[0], upper_coupling.reshape(16, 64, 64)
    )
    return run_field(
        near_lists.T, near_counts, far_lists.T, coupling, transfer, basis, rhs, win, cwin, pts, local
    )


def solution(mesh):
    return jax.shard_map(
        per_device,
        mesh=mesh,
        in_specs=(
            P(None, "leaf"),
            P(None, "leaf"),
            P("leaf", None, None),
            P("leaf", None, None),
            P("leaf", None, None, None),
            P("leaf", None, None, None, None),
            P("leaf", None, None, None),
            P("leaf", None),
            P("leaf"),
            P("leaf", None),
        ),
        out_specs=P(None, "leaf"),
        check_vma=False,
    )
```

```python
import functools
import math

import jax
import jax.numpy as jnp
from jax import lax
from jax.experimental import pallas as pl
from jax.experimental.pallas import tpu as pltpu
from jax.sharding import PartitionSpec as P

LOG2_E = math.log2(math.e)
SQ_RATE = 75.0
NOISE = 0.1
OFFSETS = (-3, -2, 2, 3)
HALO = (-2, -1, 1, 2)
LEAVES = 40
PAIRS = LEAVES // 2
SLOTS = 27
LEVELS = 4
BATCH = 8
COEF_UNROLL = 10
HALO_CUT = 26
TINY = 1e-12
MESH = pl.DeviceIdType.MESH
bf16 = jnp.bfloat16
f32 = jnp.float32
NT = (((1,), (1,)), ((), ()))


def rounded(x):
    return x.astype(bf16).astype(f32)


def dot(a, b):
    return jnp.dot(a, b, preferred_element_type=f32)


def dot_nt(a, b):
    return lax.dot_general(a, b, NT, preferred_element_type=f32)


def norm_pieces(c):
    sq = c * c
    n2 = SQ_RATE * (sq[0:1] + sq[1:2] + sq[2:3])
    high = rounded(n2)
    mid = rounded(n2 - high)
    low = n2 - high - mid
    return high, mid, low


def comm_kernel(
    coords_h,
    rhs_h,
    basis_h,
    transfer_h,
    up_t_h,
    up_c_h,
    win,
    cwin,
    pts_h,
    local_h,
    coords,
    rhs,
    basis,
    transfer,
    up_t,
    up_c,
    load_sems,
    own,
    cown,
    pts,
    local,
    blank,
    store_sems,
    blank_sems,
    tsend,
    trecv,
    lev,
    lrecv,
    halo_send,
    halo_recv,
    term_send,
    term_recv,
    lev_send,
    lev_recv,
):
    n = lax.axis_size("leaf")
    me = lax.axis_index("leaf")
    pairs = [
        (coords_h, coords),
        (rhs_h, rhs),
        (basis_h, basis),
        (transfer_h, transfer),
        (up_t_h, up_t),
        (up_c_h, up_c),
    ]
    loads = [pltpu.make_async_copy(a, b, load_sems.at[num]) for num, (a, b) in enumerate(pairs)]
    for load in loads:
        load.start()

    def away(k):
        return lax.rem(me + k + n, n)

    def partner(m):
        bits = [lax.rem(me, 2), lax.rem(me // 2, 2), lax.rem(me // 4, 2)]
        other = me
        for b in range(3):
            if m >> b & 1:
                other = other + (1 - 2 * bits[b]) * (1 << b)
        return other

    def inside(k):
        return jnp.logical_and(me + k >= 0, me + k < n)

    steps = sorted({2} | {abs(o) << j for j in range(LEVELS) for o in OFFSETS})
    steps = steps + [-k for k in steps]
    lrecv[...] = jnp.zeros_like(lrecv)
    barrier = pltpu.get_barrier_semaphore()
    for m in range(1, 8):
        pl.semaphore_signal(barrier, inc=1, device_id=(partner(m),), device_id_type=MESH)
    greeted = jnp.int32(7)
    for k in steps:
        greeted = greeted + jnp.where(inside(k), 1, 0)

        @pl.when(inside(k))
        def _(k=k):
            pl.semaphore_signal(barrier, inc=1, device_id=(away(k),), device_id_type=MESH)

    ones2 = jnp.ones((2, 128), f32)
    ones3 = jnp.ones((3, 128), f32)
    zero8 = jnp.zeros((8, 128), f32)
    zero3 = jnp.zeros((3, 128), f32)
    zero1 = jnp.zeros((1, 128), f32)

    def build(i, carry):
        at = pl.ds(pl.multiple_of(i * 128, 128), 128)
        c = coords[:, at].astype(f32)
        high, mid, low = norm_pieces(c)
        tile = jnp.concatenate([rhs[:, at], c, high, mid, low, ones2], axis=0)
        own[i] = tile.astype(bf16)
        return carry

    for load in loads[:2]:
        load.wait()
    lax.fori_loop(0, LEAVES, build, 0, unroll=4)

    lane = lax.broadcasted_iota(jnp.int32, (8, 128), 1)

    def coef_four(u, total):
        halves = []
        for h in range(2):
            t = 2 * u + h
            at = pl.ds(pl.multiple_of(t * 256, 256), 256)
            r = rhs[:, at]
            both = jnp.concatenate([r[:, :128], r[:, 128:]], axis=0).astype(bf16)
            x = dot_nt(both, basis[t])
            pair = jnp.where(lane < 64, x[:8], x[8:])
            halves.append(pair)
            total = total + dot(pair.astype(bf16), transfer[t])
        cown[u] = jnp.concatenate(halves, axis=0).astype(bf16)
        return total

    for load in loads[2:]:
        load.wait()
    level_zero = lax.fori_loop(0, PAIRS // 2, coef_four, jnp.zeros((8, 64), f32), unroll=COEF_UNROLL)
    zero64 = jnp.zeros((8, 64), f32)

    def widen(x):
        return jnp.concatenate([x, zero64], axis=1)

    half = level_zero.astype(bf16)
    lev[0] = widen(half.astype(f32))
    for j in range(3):
        tsend[2 - j] = widen(dot(half, up_t[j]))

    blank[...] = jnp.zeros_like(blank)
    stores = [
        pltpu.make_async_copy(own, win.at[pl.ds(2 * LEAVES, LEAVES)], store_sems.at[0]),
        pltpu.make_async_copy(cown, cwin.at[pl.ds(PAIRS, PAIRS // 2)], store_sems.at[1]),
    ]
    for store in stores:
        store.start()

    def clears(num, k):
        return (
            pltpu.make_async_copy(
                blank, win.at[pl.ds((2 + k) * LEAVES, LEAVES)], blank_sems.at[num, 0]
            ),
            pltpu.make_async_copy(
                blank.at[pl.ds(0, PAIRS // 2)],
                cwin.at[pl.ds((2 + k) * (PAIRS // 2), PAIRS // 2)],
                blank_sems.at[num, 1],
            ),
        )

    for num, k in enumerate(HALO):
        @pl.when(jnp.logical_not(inside(k)))
        def _(num=num, k=k):
            for clear in clears(num, k):
                clear.start()

    pl.semaphore_wait(barrier, greeted)

    terms = []
    for m in range(1, 8):
        count = 3 if m == 1 else 2 if m < 4 else 1
        terms.append(
            pltpu.make_async_remote_copy(
                src_ref=tsend.at[pl.ds(0, count)],
                dst_ref=trecv.at[m, pl.ds(0, count)],
                send_sem=term_send.at[m],
                recv_sem=term_recv.at[m],
                device_id=(partner(m),),
                device_id_type=MESH,
            )
        )
        terms[-1].start()

    copies = []

    def begin(k, copy):
        copies.append((k, copy))

        @pl.when(inside(k))
        def _():
            copy.start()

    def finish(some):
        for k, copy in some:
            @pl.when(inside(k))
            def _(copy=copy):
                copy.wait_send()

            @pl.when(inside(-k))
            def _(copy=copy):
                copy.wait_recv()

    def send_level(j):
        for num, o in enumerate(OFFSETS):
            k = -o * 2**j
            copy = pltpu.make_async_remote_copy(
                src_ref=lev.at[j],
                dst_ref=lrecv.at[j, num],
                send_sem=lev_send.at[j, num],
                recv_sem=lev_recv.at[j, num],
                device_id=(away(k),),
                device_id_type=MESH,
            )
            begin(k, copy)

    send_level(0)
    core = lax.rem(me, 2)
    sibling = me + 1 - 2 * core
    chunks = [
        (own, win, LEAVES, 0, HALO_CUT),
        (own, win, LEAVES, HALO_CUT, LEAVES - HALO_CUT),
        (cown, cwin, PAIRS // 2, 0, PAIRS // 2),
    ]

    def halo_copy(route, part, src, slot, device):
        _, ref, rows, at, size = chunks[part]
        return pltpu.make_async_remote_copy(
            src_ref=src,
            dst_ref=ref.at[pl.ds(slot * rows + at, size)],
            send_sem=halo_send.at[route, part],
            recv_sem=halo_recv.at[route, part],
            device_id=(device,),
            device_id_type=MESH,
        )

    outer = {}
    to_sibling = []

    def send_halo(part):
        mine, _, _, at, size = chunks[part]
        src = mine.at[pl.ds(at, size)]
        for route, k in enumerate((-2, 2)):
            copy = halo_copy(route, part, src, 2 - k, away(k))
            outer[k, part] = copy

            @pl.when(inside(k))
            def _(copy=copy):
                copy.start()

        to_sibling.append(halo_copy(2, part, src, 1 + 2 * core, sibling))
        to_sibling[-1].start()

    send_halo(2)
    send_halo(0)

    for copy in terms:
        copy.wait()
    for j in (1, 2, 3):
        total = tsend[3 - j]
        for m in range(1, 2**j):
            total = total + trecv[m, 3 - j]
        lev[j] = rounded(total)
        send_level(j)

    send_halo(1)

    def build_points(i, carry):
        at = pl.ds(pl.multiple_of(i * 128, 128), 128)
        c = coords[:, at].astype(f32)
        high, mid, low = norm_pieces(c)
        whole = (-2.0 * SQ_RATE) * c
        main = rounded(whole)
        rows = [zero8, main, ones3, high, mid, zero8, whole - main, zero3, low, zero1]
        tile = jnp.concatenate(rows, axis=0)
        pts[i] = tile.T.astype(bf16)
        return carry

    lax.fori_loop(0, LEAVES, build_points, 0, unroll=4)
    stores.append(pltpu.make_async_copy(pts, pts_h, store_sems.at[2]))
    stores[-1].start()

    forwards = {}

    def forward_halo(part):
        _, ref, rows, at, size = chunks[part]
        src = ref.at[pl.ds((4 - 4 * core) * rows + at, size)]
        copy = halo_copy(3, part, src, 3 - 2 * core, sibling)
        forwards[part] = copy

        @pl.when(jnp.logical_and(core == 0, inside(2)))
        def _():
            outer[-2, part].wait_recv()
            copy.start()

        @pl.when(jnp.logical_and(core == 1, inside(-2)))
        def _():
            outer[2, part].wait_recv()
            copy.start()

    forward_halo(2)
    forward_halo(0)
    forward_halo(1)
    finish(copies)
    total = jnp.zeros((8, 64), f32)
    for j in range(LEVELS):
        for num in range(4):
            coef = lrecv[j, num][:, :64]
            total = total + dot(coef.astype(bf16), up_c[4 * j + num])
    local[...] = total
    stores.append(pltpu.make_async_copy(local, local_h, store_sems.at[3]))
    stores[-1].start()
    for store in stores:
        store.wait()
    for num, k in enumerate(HALO):
        @pl.when(jnp.logical_not(inside(k)))
        def _(num=num, k=k):
            for clear in clears(num, k):
                clear.wait()

    for copy in to_sibling:
        copy.wait()
    for part in range(3):
        for k in (-2, 2):
            @pl.when(inside(k))
            def _(copy=outer[k, part]):
                copy.wait_send()

        @pl.when(jnp.logical_and(core == 1, inside(2)))
        def _(copy=outer[-2, part]):
            copy.wait_recv()

        @pl.when(jnp.logical_and(core == 0, inside(-2)))
        def _(copy=outer[2, part]):
            copy.wait_recv()

        @pl.when(inside(2 - 4 * core))
        def _(copy=forwards[part]):
            copy.wait_send()

        @pl.when(inside(2 * core - 1))
        def _(copy=forwards[part]):
            copy.wait_recv()


def matern(u):
    u = jnp.maximum(u, TINY)
    x = u * lax.rsqrt(u)
    return ((1.0 + x) * jnp.exp2(-LOG2_E * x)).astype(bf16)


def expand_coefs(cwin, table, first):
    def expand(t, carry):
        x = cwin[t].astype(f32)
        y = pltpu.roll(x, 64, 1)
        for h in range(2):
            a, b = x[8 * h : 8 * h + 8], y[8 * h : 8 * h + 8]
            table[4 * t + 2 * h] = jnp.where(first, a, b)
            table[4 * t + 2 * h + 1] = jnp.where(first, b, a)
        return carry

    lax.fori_loop(0, 5 * PAIRS // 2, expand, 0, unroll=5)


def far_stage(fars, cwin, local, coupling, transfer, basis, rhs, out, table, held):
    first = lax.broadcasted_iota(jnp.int32, (8, 128), 1) < 64
    expand_coefs(cwin, table, first)
    local_half = local[...].astype(bf16)

    def far_sums(t):
        sums = []
        for h in range(2):
            i = 2 * t + h
            cols = [
                jnp.where(first, table[fars[2 * m, i]], table[fars[2 * m + 1, i]]) for m in range(4)
            ]
            x = jnp.concatenate(cols, axis=1).astype(bf16)
            sums.append(dot(x, coupling[i]))
        both = jnp.concatenate(sums, axis=1) + dot_nt(local_half, transfer[t])
        held[...] = rounded(both)

    def far_field(t):
        both = held[...]
        zero = jnp.zeros_like(both)
        split = jnp.concatenate([jnp.where(first, both, zero), jnp.where(first, zero, both)], axis=0)
        far = dot(split.astype(bf16), basis[t])
        for h in range(2):
            at = pl.ds(pl.multiple_of(t * 256 + h * 128, 128), 128)
            out[:, at] += far[8 * h : 8 * h + 8] + NOISE * rhs[:, at]

    return far_sums, far_field


def field_phase(lists, counts, win, pts, out, dist, block, prepare_far):
    out[...] = jnp.zeros_like(out)
    nothing = jnp.zeros((16, 128), bf16)

    def advance(leaf, s):
        n = counts[jnp.minimum(leaf, LEAVES - 1)]
        last = s + 2 >= n
        return jnp.where(last, leaf + 1, leaf), jnp.where(last, 0, s + 2)

    def batch_from(leaf, s):
        batch = []
        for _ in range(BATCH):
            batch.append((leaf, s))
            leaf, s = advance(leaf, s)
        return batch, leaf, s

    def entries(leaf, s):
        i = jnp.minimum(leaf, LEAVES - 1)
        return i, lists[s, i], lists[jnp.minimum(s + 1, SLOTS - 1), i]

    def distance(leaf, s, g):
        i, a, b = entries(leaf, s)
        q = jnp.concatenate([win[a], win[b]], axis=1)
        dist[g] = dot(pts[i], jnp.concatenate([q, q], axis=0))

    def values(g):
        block[g] = matern(dist[g])

    def product(leaf, s, g):
        i, a, b = entries(leaf, s)
        live = leaf < LEAVES
        both = jnp.logical_and(live, s + 1 < counts[i])
        ra = jnp.where(live, win[a], nothing)
        rb = jnp.where(both, win[b], nothing)
        r = jnp.concatenate([ra, rb], axis=1)
        k = block[g]
        d = dot_nt(r, k)
        at = pl.ds(pl.multiple_of(i * 128, 128), 128)
        out[:, at] += d[:8]

    tasks = lax.fori_loop(0, LEAVES, lambda i, t: t + (counts[i] + 1) // 2, jnp.int32(0))
    zero = jnp.int32(0)
    now, leaf, s = batch_from(zero, zero)
    for g in range(BATCH):
        distance(*now[g], g)
    mid, leaf, s = batch_from(leaf, s)
    for g in range(BATCH):
        values(g)
        distance(*mid[g], g)

    def near_step(carry, extra=None):
        now, mid, leaf, s = carry
        later, leaf, s = batch_from(leaf, s)
        for g in range(BATCH):
            if extra and g in extra:
                extra[g]()
            product(*now[g], g)
            values(g)
            distance(*later[g], g)
        return mid, later, leaf, s

    rounds = (tasks + BATCH - 1) // BATCH
    shared = jnp.minimum(rounds, PAIRS)
    carry = lax.fori_loop(0, rounds - shared, lambda _, c: near_step(c), (now, mid, leaf, s))
    far_sums, far_field = prepare_far()

    def both_steps(t, carry):
        return near_step(carry, {0: lambda: far_sums(t), 6: lambda: far_field(t)})

    def far_step(t, carry):
        far_sums(t)
        far_field(t)
        return carry

    lax.fori_loop(0, shared, both_steps, carry)
    lax.fori_loop(shared, PAIRS, far_step, 0)


def field_kernel(
    lists_h,
    counts_h,
    fars_h,
    coupling_h,
    transfer_h,
    basis_h,
    rhs_h,
    win_h,
    cwin_h,
    pts_h,
    local_h,
    out,
    lists,
    counts,
    fars,
    coupling,
    transfer,
    basis,
    rhs,
    win,
    cwin,
    pts,
    local,
    sems,
    table,
    held,
    dist,
    block,
):
    pairs = [
        (lists_h, lists),
        (counts_h, counts),
        (win_h, win),
        (pts_h, pts),
        (fars_h, fars),
        (cwin_h, cwin),
        (local_h, local),
        (coupling_h, coupling),
        (transfer_h, transfer),
        (basis_h, basis),
        (rhs_h, rhs),
    ]
    copies = [pltpu.make_async_copy(a, b, sems.at[n]) for n, (a, b) in enumerate(pairs)]
    for copy in copies[:4]:
        copy.start()
    for copy in copies[:4]:
        copy.wait()
    for copy in copies[4:]:
        copy.start()
    def prepare_far():
        for copy in copies[4:]:
            copy.wait()
        return far_stage(fars, cwin, local, coupling, transfer, basis, rhs, out, table, held)

    field_phase(lists, counts, win, pts, out, dist, block, prepare_far)


def run_field(lists, counts, fars, coupling, transfer, basis, rhs, *arrays):
    hbm = pl.BlockSpec(memory_space=pltpu.HBM)
    vmem = pl.BlockSpec(memory_space=pltpu.VMEM)
    return pl.pallas_call(
        field_kernel,
        out_shape=jax.ShapeDtypeStruct((8, LEAVES * 128), f32),
        in_specs=[hbm] * (7 + len(arrays)),
        out_specs=vmem,
        scratch_shapes=[
            pltpu.SMEM((SLOTS, LEAVES), jnp.int32),
            pltpu.SMEM((LEAVES,), jnp.int32),
            pltpu.SMEM((8, LEAVES), jnp.int32),
            pltpu.VMEM((LEAVES, 512, 64), bf16),
            pltpu.VMEM((PAIRS, 128, 64), bf16),
            pltpu.VMEM((PAIRS, 128, 128), bf16),
            pltpu.VMEM((8, LEAVES * 128), f32),
            *[pltpu.VMEM(x.shape, x.dtype) for x in arrays],
            pltpu.SemaphoreType.DMA((11,)),
            pltpu.VMEM((5 * LEAVES, 8, 128), f32),
            pltpu.VMEM((8, 128), f32),
            pltpu.VMEM((BATCH, 128, 256), f32),
            pltpu.VMEM((BATCH, 128, 256), bf16),
        ],
        compiler_params=pltpu.CompilerParams(vmem_limit_bytes=60 * 2**20),
    )(lists, counts, fars, coupling, transfer, basis, rhs, *arrays)


def run_comm(*arrays):
    hbm = pl.BlockSpec(memory_space=pltpu.HBM)
    dma = pltpu.SemaphoreType.DMA
    return pl.pallas_call(
        comm_kernel,
        out_shape=[
            jax.ShapeDtypeStruct((5 * LEAVES, 16, 128), bf16),
            jax.ShapeDtypeStruct((5 * PAIRS // 2, 16, 128), bf16),
            jax.ShapeDtypeStruct((LEAVES, 128, 32), bf16),
            jax.ShapeDtypeStruct((8, 64), f32),
        ],
        in_specs=[hbm] * len(arrays),
        out_specs=[hbm] * 4,
        scratch_shapes=[pltpu.VMEM(x.shape, x.dtype) for x in arrays]
        + [
            dma((6,)),
            pltpu.VMEM((LEAVES, 16, 128), bf16),
            pltpu.VMEM((PAIRS // 2, 16, 128), bf16),
            pltpu.VMEM((LEAVES, 128, 32), bf16),
            pltpu.VMEM((8, 64), f32),
            pltpu.VMEM((LEAVES, 16, 128), bf16),
            dma((4,)),
            dma((4, 2)),
            pltpu.VMEM((3, 8, 128), f32),
            pltpu.VMEM((8, 3, 8, 128), f32),
            pltpu.VMEM((LEVELS, 8, 128), f32),
            pltpu.VMEM((LEVELS, 4, 8, 128), f32),
            dma((4, 3)),
            dma((4, 3)),
            dma((8,)),
            dma((8,)),
            dma((LEVELS, 4)),
            dma((LEVELS, 4)),
        ],
        compiler_params=pltpu.CompilerParams(
            collective_id=0, has_side_effects=True, vmem_limit_bytes=60 * 2**20
        ),
    )(*arrays)


def per_device(
    coords,
    rhs,
    leaf_basis,
    leaf_transfer,
    upper_transfer,
    upper_coupling,
    leaf_coupling,
    near_lists,
    near_counts,
    far_lists,
):
    basis = leaf_basis.reshape(PAIRS, 128, 128)
    transfer = leaf_transfer.reshape(PAIRS, 128, 64)
    coupling = leaf_coupling.reshape(LEAVES, 512, 64)
    win, cwin, pts, local = run_comm(
        coords, rhs, basis, transfer, upper_transfer[0], upper_coupling.reshape(16, 64, 64)
    )
    return run_field(
        near_lists.T, near_counts, far_lists.T, coupling, transfer, basis, rhs, win, cwin, pts, local
    )


def solution(mesh):
    return jax.shard_map(
        per_device,
        mesh=mesh,
        in_specs=(
            P(None, "leaf"),
            P(None, "leaf"),
            P("leaf", None, None),
            P("leaf", None, None),
            P("leaf", None, None, None),
            P("leaf", None, None, None, None),
            P("leaf", None, None, None),
            P("leaf", None),
            P("leaf"),
            P("leaf", None),
        ),
        out_specs=P(None, "leaf"),
        check_vma=False,
    )
```
